768 devices in a mesh: group: 16 (over y, core), dom: 48 (over z, x).
Axes of the slice: x: 4, y: 8, z: 12, core: 2. Of those that a mesh axis runs over, the one named last changes fastest.
Arguments:
- prior: bfloat16 [294912, 1000], P(('group', 'dom')), may hold values from 0.019897461 to 2
- seed_labels: int32 [294912], P(('group', 'dom')), may hold values from 0 to 3999
- degree: int32 [294912], P(('group', 'dom')), may hold values from 42 to 85
- tiles: bfloat16 [2304, 8, 128, 128], P(('group', 'dom')), may hold values from 0 to 1, as said below
- tile_source: int32 [2304, 8], P(('group', 'dom')), may hold values from 0 to 8, as said below
- tile_count: int32 [768], P(('group', 'dom')), may hold values from 8 to 24
- send_list: int32 [768, 6], P(('group', 'dom')), may hold values from 0 to 2
Outputs:
- labels: float32 [294912, 1000], P(('group', 'dom'))
The draws below stay inside these ranges and needn't reach their ends.
Inputs may be any that keep to these rules, and one draw needn't show every extreme that they name: `seed_labels`: a value below 1000 seeds that class; larger values leave the node unseeded. Only the first tile_count slots of a device, row block after row block, hold live tiles. `tiles`: nonnegative edge weights, most of them zero. `tile_source`: index of a source slot.
All inputs are finite; a program needn't handle non-finite values.
Results may differ from the reference program's by a relative error of at most 0.00032.
Values may be sent and summed in bfloat16 or wider, within the bound.
No kernel may reach another device: no remote copies, remote signals or barrier semaphores. Data moves between devices by JAX's collectives and lax.ppermute only.
A program may use at most 32 MiB of HBM per device.

```python
import math
import jax
import jax.numpy as jnp
from jax import lax

C = 1000
BLK = 128
RB = 3
TPR = 8
ITERS = 3
NSRC = 9
NTILES = 2304
NODES = 294912
N_GROUP = 16
N_DOM = 48


def draw_tiles(key, part):
    key = jax.random.fold_in(key, 11)
    key_mask, key_value = jax.random.split(key)
    shape = (NTILES, TPR, BLK, BLK)
    density = 1.0 / 8.0
    values = jnp.exp(jax.random.uniform(key_value, shape, jnp.float32, jnp.log(0.25), 0.0))
    keep = jax.random.uniform(key_mask, shape, jnp.float32) < density
    return jnp.where(keep, values, 0.0).astype(jnp.bfloat16)


def draw_tile_source(key, part):
    key = jax.random.fold_in(key, 23)
    key_head, key_rest, key_perm = jax.random.split(key, 3)
    devices_all = NTILES // RB
    slots_all = RB * TPR
    leading = max(6, slots_all // 3)
    head = jax.random.randint(key_head, (devices_all, leading), 0, NSRC, dtype=jnp.int32)
    fixed = RB + jnp.arange(6, dtype=jnp.int32)
    head = head.at[:, :6].set(jnp.broadcast_to(fixed, (devices_all, 6)))
    perm_keys = jax.random.split(key_perm, devices_all)
    orders = jax.vmap(lambda k: jax.random.permutation(k, leading))(perm_keys)
    head = jnp.take_along_axis(head, orders.astype(jnp.int32), axis=1)
    rest = jax.random.randint(key_rest, (devices_all, slots_all - leading), 0, NSRC, dtype=jnp.int32)
    whole = jnp.concatenate([head, rest], axis=1)
    return whole.reshape(NTILES, TPR).astype(jnp.int32)


def touch_ends(result, key, low, largest):
    shape = result.shape
    index_at = [jax.random.randint(jax.random.fold_in(key, axis), (), 0, shape[axis]) for axis in range(len(shape))]
    result = result.at[tuple(index_at)].set(low)
    longest = shape.index(max(shape))
    index_at[longest] = (index_at[longest] + 1) % shape[longest]
    return result.at[tuple(index_at)].set(largest)


def block_scale(key, dims, pieces, smallest, largest):
    def one(position, parts):
        steps = jax.random.uniform(jax.random.fold_in(jax.random.fold_in(key, 6), position), (parts,), jnp.float32, smallest / len(pieces), largest / len(pieces))
        return jnp.repeat(jnp.exp(steps), dims[position] // parts).reshape((-1,) + (1,) * (len(dims) - position - 1))

    gain = one(*pieces[0])
    for cut in pieces[1:]:
        gain = gain * one(*cut)
    return gain


def setup_inputs(seed: int = 0) -> dict:
    keys = jax.random.split(jax.random.key(seed), 8)
    prior = jnp.clip(jnp.exp(math.log(2.0) - 4.61031033 * jax.random.uniform(keys[0], (NODES, C), jnp.float32) ** block_scale(keys[0], (NODES, C), ((0, 768),), -0.2, 0.2)), 0.019897461, 2.0).astype(jnp.bfloat16)
    seed_labels = touch_ends(jax.random.randint(keys[1], (NODES,), 0, 4 * C), jax.random.fold_in(keys[1], 1), 0, (4 * C) - 1).astype(jnp.int32)
    degree = touch_ends(jax.random.randint(keys[2], (NODES,), max(1, TPR * BLK // 24), TPR * BLK // 12 + 1), jax.random.fold_in(keys[2], 1), max(1, TPR * BLK // 24), (TPR * BLK // 12 + 1) - 1).astype(jnp.int32)
    tiles = draw_tiles(jax.random.fold_in(keys[7], 71), 0)
    tile_source = draw_tile_source(jax.random.fold_in(keys[7], 71), 0)
    tile_count = touch_ends(jax.random.randint(keys[5], (N_GROUP * N_DOM,), max(6, RB * TPR // 3), RB * TPR + 1), jax.random.fold_in(keys[5], 1), max(6, RB * TPR // 3), RB * TPR).astype(jnp.int32)
    send_list = touch_ends(jax.random.randint(keys[6], (N_GROUP * N_DOM, 6), 0, RB), jax.random.fold_in(keys[6], 1), 0, RB - 1).astype(jnp.int32)
    return dict(prior=prior, seed_labels=seed_labels, degree=degree, tiles=tiles, tile_source=tile_source, tile_count=tile_count, send_list=send_list)


def spread_product(scaled, send_list, tiles, tile_source, tile_count):
    grid = scaled.reshape(N_GROUP, N_DOM, RB, BLK, C)
    sends = send_list.reshape(N_GROUP, N_DOM, 6)
    tile_grid = tiles.reshape(N_GROUP * N_DOM, RB, TPR, BLK, BLK)
    source_grid = tile_source.reshape(N_GROUP * N_DOM, RB, TPR)

    def fetch(grp, dmn, column):
        valid = (grp >= 0) & (grp < N_GROUP) & (dmn >= 0) & (dmn < N_DOM)
        grp_c = jnp.clip(grp, 0, N_GROUP - 1).astype(jnp.int32)
        dmn_c = jnp.clip(dmn, 0, N_DOM - 1).astype(jnp.int32)
        which = sends[grp_c, dmn_c, column].astype(jnp.int32)
        block = grid[grp_c, dmn_c, which]
        return jnp.where(valid, block, jnp.zeros_like(block))

    def one_device(items):
        flat, tile_dev, source_dev, count = items
        grp = flat // N_DOM
        dmn = flat % N_DOM
        local = grid[grp, dmn]
        received = jnp.stack([fetch(grp, dmn - 1, 1), fetch(grp, dmn + 1, 0), fetch(grp, dmn - 2, 3), fetch(grp, dmn + 2, 2), fetch(grp - 1, dmn, 5), fetch(grp + 1, dmn, 4)])
        sources = jnp.concatenate([local, received], axis=0).astype(jnp.float32)
        live = jnp.arange(RB * TPR).reshape(RB, TPR) < count
        weights = jnp.where(live[:, :, None, None], tile_dev.astype(jnp.float32), 0.0)
        select = (source_dev[:, :, None] == jnp.arange(NSRC)[None, None, :]).astype(jnp.float32)
        combined = jnp.einsum('rtij,rts->risj', weights, select).astype(jnp.bfloat16)
        return jnp.einsum('risj,sjc->ric', combined.astype(jnp.float32), sources).reshape(RB * BLK, C)
    flats = jnp.arange(N_GROUP * N_DOM, dtype=jnp.int32)
    out = lax.map(one_device, (flats, tile_grid, source_grid, tile_count))
    return out.reshape(NODES, C)

def reference(prior, seed_labels, degree, tiles, tile_source, tile_count, send_list):
    onehot = (seed_labels[:, None] == jnp.arange(C)[None, :]).astype(jnp.float32)
    start = jnp.where(seed_labels[:, None] < C, onehot, prior.astype(jnp.float32))
    inv_root = 1.0 / jnp.sqrt(degree.astype(jnp.float32))
    labels = start
    for step in range(ITERS):
        scaled = (inv_root[:, None] * labels).astype(jnp.bfloat16)
        product = spread_product(scaled, send_list, tiles, tile_source, tile_count)
        labels = 0.9 * inv_root[:, None] * product + 0.1 * start
    return labels
```

```python
import functools

import jax
import jax.numpy as jnp
from jax import lax
from jax.experimental import pallas as pl
from jax.experimental.pallas import tpu as pltpu
from jax.sharding import PartitionSpec as P

ITERS = 3
ROWS = 256
SMEM = pl.BlockSpec(memory_space=pltpu.SMEM)

SWAPS = (
    ("dom", 2, 0),
    ("dom", 2, 1),
    ("dom", 1, 0),
    ("dom", 1, 1),
    ("group", 1, 1),
    ("group", 1, 0),
)
UP_COLUMN = {("dom", 1): 1, ("dom", 2): 3, ("group", 1): 5}
DOWN_COLUMN = {("dom", 1): 0, ("dom", 2): 2, ("group", 1): 4}
FROM_DOWN = {("dom", 1): 0, ("dom", 2): 2, ("group", 1): 4}
FROM_UP = {("dom", 1): 1, ("dom", 2): 3, ("group", 1): 5}


def is_lower(swap):
    axis, distance, phase = swap
    return (lax.axis_index(axis) // distance) % 2 == phase


def exchange(block, swap):
    axis, distance, phase = swap
    count = lax.axis_size(axis)
    lower = [i for i in range(count - distance) if (i // distance) % 2 == phase]
    pairs = [(i, i + distance) for i in lower] + [(i + distance, i) for i in lower]
    return lax.ppermute(block, axis, pairs)


def first_labels(prior, seeds, row0):
    rows, nodes = prior.shape
    label = lax.broadcasted_iota(jnp.int32, (rows, nodes), 0) + row0
    onehot = jnp.where(label == seeds, 1.0, 0.0)
    return onehot, prior.astype(jnp.float32)


def start_of(prior_ref, seeds_ref, classes):
    seeds = seeds_ref[...]
    onehot, soft = first_labels(prior_ref[...], seeds, pl.program_id(0) * prior_ref.shape[0])
    return jnp.where(seeds < classes, onehot, soft)


def put_scaled(scaled, which_ref, own_ref, send_refs):
    own_ref[...] = scaled
    for k, ref in enumerate(send_refs):
        ref[...] = own_ref[:, pl.ds(pl.multiple_of(which_ref[k] * 128, 128), 128)]


def prepare_kernel(classes, which_ref, prior_ref, seeds_ref, degree_ref, own_ref, *send_refs):
    inv_root = 1.0 / jnp.sqrt(degree_ref[...].astype(jnp.float32))
    start = start_of(prior_ref, seeds_ref, classes)
    put_scaled((inv_root * start).astype(jnp.bfloat16), which_ref, own_ref, send_refs)


def step_kernel(
    classes, last, which_ref, prior_ref, seeds_ref, degree_ref, weight_ref, own_ref, *refs
):
    received, outs = refs[: len(SWAPS)], refs[len(SWAPS) :]
    inv_root = 1.0 / jnp.sqrt(degree_ref[...].astype(jnp.float32))
    sources = jnp.concatenate([own_ref[...]] + [ref[...] for ref in received], axis=1)
    product = jnp.dot(sources, weight_ref[...], preferred_element_type=jnp.float32)
    start = start_of(prior_ref, seeds_ref, classes)
    labels = 0.9 * inv_root * product + 0.1 * start
    if last:
        outs[0][...] = labels
    else:
        put_scaled((inv_root * labels).astype(jnp.bfloat16), which_ref, outs[0], outs[1:])


def weight_kernel(place_ref, source_ref, count_ref, tiles_ref, weight_ref, total_ref):
    row_blocks, per_row, side, _ = tiles_ref.shape
    slots = weight_ref.shape[0] // side
    for r in range(row_blocks):
        total_ref[...] = jnp.zeros_like(total_ref)
        for t in range(per_row):
            place = place_ref[source_ref[r, t]]
            live = r * per_row + t < count_ref[0]

            @pl.when(live)
            def _():
                total_ref[place] += tiles_ref[r, t].astype(jnp.float32)

        for s in range(slots):
            weight_ref[pl.ds(s * side, side), pl.ds(r * side, side)] = total_ref[s].T.astype(
                weight_ref.dtype
            )


def on_device(prior, seed_labels, degree, tiles, tile_source, tile_count, send_list):
    row_blocks, per_row, side, _ = tiles.shape
    nodes, classes = prior.shape
    slots = row_blocks + len(SWAPS)
    prior_t = prior.T
    seeds = seed_labels[None, :]
    degrees = degree[None, :]

    which, place = [], list(range(row_blocks)) + [0] * len(SWAPS)
    for k, swap in enumerate(SWAPS):
        lower, kind = is_lower(swap), swap[:2]
        which.append(jnp.where(lower, send_list[0, UP_COLUMN[kind]], send_list[0, DOWN_COLUMN[kind]]))
        mate = [other for other in SWAPS if other[:2] == kind and other != swap][0]
        other = SWAPS.index(mate)
        place[row_blocks + FROM_UP[kind]] = jnp.where(lower, row_blocks + k, row_blocks + other)
        place[row_blocks + FROM_DOWN[kind]] = jnp.where(lower, row_blocks + other, row_blocks + k)
    which = jnp.stack(which).astype(jnp.int32)
    place = jnp.stack([jnp.asarray(p, jnp.int32) for p in place])

    grid = (pl.cdiv(classes, ROWS),)
    wide = pl.BlockSpec((ROWS, nodes), lambda i: (i, 0))
    narrow = pl.BlockSpec((ROWS, side), lambda i: (i, 0))
    lanes = pl.BlockSpec((1, nodes), lambda i: (0, 0))
    weights = pl.BlockSpec((slots * side, nodes), lambda i: (0, 0))
    scaled_shapes = [jax.ShapeDtypeStruct((classes, nodes), jnp.bfloat16)] + [
        jax.ShapeDtypeStruct((classes, side), jnp.bfloat16)
    ] * len(SWAPS)
    params = pltpu.CompilerParams(vmem_limit_bytes=40 * 1024 * 1024)

    own, *sends = pl.pallas_call(
        functools.partial(prepare_kernel, classes),
        grid=grid,
        in_specs=[SMEM, wide, lanes, lanes],
        out_specs=[wide] + [narrow] * len(SWAPS),
        out_shape=scaled_shapes,
        compiler_params=params,
    )(which, prior_t, seeds, degrees)
    weight = pl.pallas_call(
        weight_kernel,
        in_specs=[SMEM, SMEM, SMEM, pl.BlockSpec(memory_space=pltpu.VMEM)],
        out_specs=pl.BlockSpec(memory_space=pltpu.VMEM),
        out_shape=jax.ShapeDtypeStruct((slots * side, nodes), jnp.bfloat16),
        scratch_shapes=[pltpu.VMEM((slots, side, side), jnp.float32)],
        compiler_params=params,
        cost_estimate=pl.CostEstimate(flops=0, bytes_accessed=8_000_000, transcendentals=0),
    )(place, tile_source, tile_count, tiles)
    for step in range(ITERS):
        last = step == ITERS - 1
        received = [exchange(block, swap) for block, swap in zip(sends, SWAPS)]
        outs = pl.pallas_call(
            functools.partial(step_kernel, classes, last),
            grid=grid,
            in_specs=[SMEM, wide, lanes, lanes, weights, wide] + [narrow] * len(SWAPS),
            out_specs=[wide] if last else [wide] + [narrow] * len(SWAPS),
            out_shape=[jax.ShapeDtypeStruct((classes, nodes), jnp.float32)] if last else scaled_shapes,
            compiler_params=params,
        )(which, prior_t, seeds, degrees, weight, own, *received)
        own, sends = outs[0], outs[1:]
    return own.T


def solution(mesh):
    return jax.shard_map(
        on_device,
        mesh=mesh,
        in_specs=(
            P(("group", "dom"), None),
            P(("group", "dom")),
            P(("group", "dom")),
            P(("group", "dom"), None, None, None),
            P(("group", "dom"), None),
            P(("group", "dom")),
            P(("group", "dom"), None),
        ),
        out_specs=P(("group", "dom"), None),
        check_vma=False,
    )
```

```python
import functools

import jax
import jax.numpy as jnp
from jax import lax
from jax.experimental import pallas as pl
from jax.experimental.pallas import tpu as pltpu
from jax.sharding import PartitionSpec as P

ITERS = 3
CORES = 2
ROW = 4
CHUNK = 256
SIDE = 128
SMEM = pl.BlockSpec(memory_space=pltpu.SMEM)
VMEM = pl.BlockSpec(memory_space=pltpu.VMEM)
HBM = pl.BlockSpec(memory_space=pltpu.HBM)
PARAMS = pltpu.CompilerParams(vmem_limit_bytes=40 * 1024 * 1024)

RING, BACK, TWO, CROSS, EDGE, UP, DOWN = range(7)
PERMUTES = 7


def routes(n_group, n_dom):
    def flat(g, d):
        return (g % n_group) * n_dom + d

    places = [(g, d) for g in range(n_group) for d in range(n_dom)]

    def ring(g, d):
        if g % CORES == 0:
            return (g, d + 1) if d % ROW < ROW - 1 else (g + 1, d)
        return (g, d - 1) if d % ROW > 0 else (g - 1, d)

    def pairs(distance, takes):
        both = []
        for g, d in places:
            if takes(d % ROW) and d + distance < n_dom:
                both += [(flat(g, d), flat(g, d + distance)), (flat(g, d + distance), flat(g, d))]
        return both

    forward = [(flat(*p), flat(*ring(*p))) for p in places]
    return {
        RING: forward,
        BACK: [(b, a) for a, b in forward],
        TWO: pairs(2, lambda x: x < 2),
        CROSS: pairs(2, lambda x: x >= 2),
        EDGE: pairs(1, lambda x: x == ROW - 1),
        UP: [(flat(g, d), flat(g + 1, d)) for g, d in places],
        DOWN: [(flat(g, d), flat(g - 1, d)) for g, d in places],
    }


def position():
    group, dom = lax.axis_index("group"), lax.axis_index("dom")
    return group, jnp.bitwise_and(group, CORES - 1), jnp.bitwise_and(dom, ROW - 1)


def columns_to_send():
    _, core, x = position()
    high = x >= 2
    return {
        RING: jnp.where(core == 0, 1, 0),
        BACK: jnp.where(core == 0, 0, 1),
        TWO: jnp.where(high, 2, 3),
        CROSS: jnp.where(high, 3, 2),
        EDGE: jnp.where(x == 0, 0, 1),
        UP: 5,
        DOWN: 4,
    }


def chunks(rows):
    return [(at, min(CHUNK, rows - at)) for at in range(0, rows, CHUNK)]


def put_sends(rows, send_ref, own_ref, send_refs):
    for k, column in columns_to_send().items():
        block = pl.ds(pl.multiple_of(send_ref[0, column] * SIDE, SIDE), SIDE)
        send_refs[k][rows, :] = own_ref[rows, block]


def prepare_kernel(send_ref, seeds_ref, degree_ref, prior_ref, start_ref, own_ref, *refs):
    send_refs, (held, arrived) = refs[:PERMUTES], refs[PERMUTES:]
    classes = prior_ref.shape[0]
    copies = []
    for k, (at, size) in enumerate(chunks(classes)):
        rows = pl.ds(at, size)
        copies.append(pltpu.make_async_copy(prior_ref.at[rows], held.at[rows], arrived.at[k]))
        copies[-1].start()
    inv_root = 1.0 / jnp.sqrt(degree_ref[...].astype(jnp.float32))
    seeds = seeds_ref[...]
    for k, (at, size) in enumerate(chunks(classes)):
        rows = pl.ds(at, size)
        copies[k].wait()
        label = lax.broadcasted_iota(jnp.int32, (size, seeds.shape[1]), 0) + at
        onehot = jnp.where(label == seeds, 1.0, 0.0)
        start = jnp.where(seeds < classes, onehot, held[rows, :].astype(jnp.float32))
        start_ref[rows, :] = start.astype(jnp.bfloat16)
        own_ref[rows, :] = (inv_root * start).astype(jnp.bfloat16)
        put_sends(rows, send_ref, own_ref, send_refs)


def new_labels(rows, degree_ref, start_ref, weight_ref, own_ref, received):
    inv_root = 1.0 / jnp.sqrt(degree_ref[...].astype(jnp.float32))
    sources = jnp.concatenate([own_ref[rows, :]] + [ref[rows, :] for ref in received], axis=1)
    product = jnp.dot(sources, weight_ref[...], preferred_element_type=jnp.float32)
    labels = 0.9 * inv_root * product + 0.1 * start_ref[rows, :].astype(jnp.float32)
    return inv_root, labels


def step_kernel(send_ref, degree_ref, start_ref, weight_ref, own_ref, *refs):
    received, next_ref, send_refs = refs[:PERMUTES], refs[PERMUTES], refs[PERMUTES + 1 :]
    for at, size in chunks(own_ref.shape[0]):
        rows = pl.ds(at, size)
        inv_root, labels = new_labels(rows, degree_ref, start_ref, weight_ref, own_ref, received)
        next_ref[rows, :] = (inv_root * labels).astype(jnp.bfloat16)
        put_sends(rows, send_ref, next_ref, send_refs)


def last_kernel(degree_ref, start_ref, weight_ref, own_ref, *refs):
    received, (out_ref, held, left) = refs[:PERMUTES], refs[PERMUTES:]
    copies = []
    for k, (at, size) in enumerate(chunks(own_ref.shape[0])):
        rows = pl.ds(at, size)
        _, labels = new_labels(rows, degree_ref, start_ref, weight_ref, own_ref, received)
        held[rows, :] = labels
        copies.append(pltpu.make_async_copy(held.at[rows], out_ref.at[rows], left.at[k]))
        copies[-1].start()
    for copy in copies:
        copy.wait()


def weight_kernel(n_group, source_ref, count_ref, tiles_ref, weight_ref, total_ref):
    row_blocks, per_row, side, _ = tiles_ref.shape
    group, core, x = position()
    own = row_blocks
    place = [
        jnp.where(x == 0, own + EDGE, jnp.where(core == 0, own + RING, own + BACK)),
        jnp.where(x == ROW - 1, own + EDGE, jnp.where(core == 0, own + BACK, own + RING)),
        jnp.where(x >= 2, own + TWO, own + CROSS),
        jnp.where(x >= 2, own + CROSS, own + TWO),
        own + UP,
        own + DOWN,
    ]
    for r in range(row_blocks):
        total_ref[...] = jnp.zeros_like(total_ref)
        for t in range(per_row):
            source = source_ref[r, t]
            slot = source
            for k, where in enumerate(place):
                slot = jnp.where(source == own + k, where, slot)
            live = r * per_row + t < count_ref[0]
            live = live & ((source != own + 4) | (group > 0))
            live = live & ((source != own + 5) | (group < n_group - 1))

            @pl.when(live)
            def _():
                total_ref[slot] += tiles_ref[r, t].astype(jnp.float32)

        for s in range(own + PERMUTES):
            weight_ref[pl.ds(s * side, side), pl.ds(r * side, side)] = total_ref[s].T.astype(
                weight_ref.dtype
            )


def on_device(prior, seed_labels, degree, tiles, tile_source, tile_count, send_list):
    row_blocks, _, side, _ = tiles.shape
    nodes, classes = prior.shape
    n_group, n_dom = lax.axis_size("group"), lax.axis_size("dom")
    route = routes(n_group, n_dom)
    slots = row_blocks + PERMUTES
    pieces = len(chunks(classes))
    seeds, degrees = seed_labels[None, :], degree[None, :]
    wide = jax.ShapeDtypeStruct((classes, nodes), jnp.bfloat16)
    narrow = [jax.ShapeDtypeStruct((classes, side), jnp.bfloat16)] * PERMUTES

    start, own, *sends = pl.pallas_call(
        prepare_kernel,
        in_specs=[SMEM, VMEM, VMEM, HBM],
        out_specs=[VMEM] * (2 + PERMUTES),
        out_shape=[wide, wide] + narrow,
        scratch_shapes=[
            pltpu.VMEM((classes, nodes), jnp.bfloat16),
            pltpu.SemaphoreType.DMA((pieces,)),
        ],
        compiler_params=PARAMS,
    )(send_list, seeds, degrees, prior.T)
    weight = pl.pallas_call(
        functools.partial(weight_kernel, n_group),
        in_specs=[SMEM, SMEM, VMEM],
        out_specs=VMEM,
        out_shape=jax.ShapeDtypeStruct((slots * side, nodes), jnp.bfloat16),
        scratch_shapes=[pltpu.VMEM((slots, side, side), jnp.float32)],
        compiler_params=PARAMS,
        cost_estimate=pl.CostEstimate(flops=0, bytes_accessed=8_000_000, transcendentals=0),
    )(tile_source, tile_count, tiles)
    for step in range(ITERS):
        received = [lax.ppermute(sends[k], ("group", "dom"), route[k]) for k in range(PERMUTES)]
        if step < ITERS - 1:
            own, *sends = pl.pallas_call(
                step_kernel,
                in_specs=[SMEM] + [VMEM] * (4 + PERMUTES),
                out_specs=[VMEM] * (1 + PERMUTES),
                out_shape=[wide] + narrow,
                compiler_params=PARAMS,
            )(send_list, degrees, start, weight, own, *received)
    labels = pl.pallas_call(
        last_kernel,
        in_specs=[VMEM] * (4 + PERMUTES),
        out_specs=HBM,
        out_shape=jax.ShapeDtypeStruct((classes, nodes), jnp.float32),
        scratch_shapes=[
            pltpu.VMEM((classes, nodes), jnp.float32),
            pltpu.SemaphoreType.DMA((pieces,)),
        ],
        compiler_params=PARAMS,
    )(degrees, start, weight, own, *received)
    return labels.T


def solution(mesh):
    return jax.shard_map(
        on_device,
        mesh=mesh,
        in_specs=(
            P(("group", "dom"), None),
            P(("group", "dom")),
            P(("group", "dom")),
            P(("group", "dom"), None, None, None),
            P(("group", "dom"), None),
            P(("group", "dom")),
            P(("group", "dom"), None),
        ),
        out_specs=P(("group", "dom"), None),
        check_vma=False,
    )
```

```python
import functools

import jax
import jax.numpy as jnp
from jax import lax
from jax.experimental import pallas as pl
from jax.experimental.pallas import tpu as pltpu
from jax.sharding import PartitionSpec as P

ITERS = 3
CORES = 2
ROW = 4
CHUNK = 256
SIDE = 128
SMEM = pl.BlockSpec(memory_space=pltpu.SMEM)
VMEM = pl.BlockSpec(memory_space=pltpu.VMEM)
HBM = pl.BlockSpec(memory_space=pltpu.HBM)
PARAMS = pltpu.CompilerParams(vmem_limit_bytes=40 * 1024 * 1024)

EDGE, RING, BACK, UP, DOWN, TWO, CROSS = range(7)
PERMUTES = 7
EARLY = 5


def routes(n_group, n_dom):
    def flat(g, d):
        return (g % n_group) * n_dom + d

    places = [(g, d) for g in range(n_group) for d in range(n_dom)]

    def ring(g, d):
        if g % CORES == 0:
            return (g, d + 1) if d % ROW < ROW - 1 else (g + 1, d)
        return (g, d - 1) if d % ROW > 0 else (g - 1, d)

    def pairs(distance, takes):
        both = []
        for g, d in places:
            if takes(d % ROW) and d + distance < n_dom:
                both += [(flat(g, d), flat(g, d + distance)), (flat(g, d + distance), flat(g, d))]
        return both

    forward = [(flat(*p), flat(*ring(*p))) for p in places]
    return {
        RING: forward,
        BACK: [(b, a) for a, b in forward],
        TWO: pairs(2, lambda x: x < 2),
        CROSS: pairs(2, lambda x: x >= 2),
        EDGE: pairs(1, lambda x: x == ROW - 1),
        UP: [(flat(g, d), flat(g + 1, d)) for g, d in places],
        DOWN: [(flat(g, d), flat(g - 1, d)) for g, d in places],
    }


def position():
    group, dom = lax.axis_index("group"), lax.axis_index("dom")
    return group, jnp.bitwise_and(group, CORES - 1), jnp.bitwise_and(dom, ROW - 1)


def columns_to_send():
    _, core, x = position()
    high = x >= 2
    return {
        RING: jnp.where(core == 0, 1, 0),
        BACK: jnp.where(core == 0, 0, 1),
        TWO: jnp.where(high, 2, 3),
        CROSS: jnp.where(high, 3, 2),
        EDGE: jnp.where(x == 0, 0, 1),
        UP: 5,
        DOWN: 4,
    }


def in_hbm(x):
    return pltpu.with_memory_space_constraint(x, pltpu.HBM)


def chunks(rows):
    return [(at, min(CHUNK, rows - at)) for at in range(0, rows, CHUNK)]


def put_sends(rows, send_ref, own_ref, send_refs):
    for k, column in columns_to_send().items():
        block = pl.ds(pl.multiple_of(send_ref[0, column] * SIDE, SIDE), SIDE)
        send_refs[k][rows, :] = own_ref[rows, block]


def prepare_kernel(send_any, seeds_any, degree_any, prior_any, root_ref, start_ref, own_ref, *refs):
    send_refs, (sends, seeds_held, degree_held, held, small, arrived) = refs[:PERMUTES], refs[PERMUTES:]
    classes = prior_any.shape[0]
    firsts = [
        pltpu.make_async_copy(seeds_any, seeds_held, small.at[0]),
        pltpu.make_async_copy(degree_any, degree_held, small.at[1]),
        pltpu.make_async_copy(send_any, sends, small.at[2]),
    ]
    copies = []
    for k, (at, size) in enumerate(chunks(classes)):
        rows = pl.ds(at, size)
        copies.append(pltpu.make_async_copy(prior_any.at[rows], held.at[rows], arrived.at[k]))
    for copy in firsts + copies:
        copy.start()
    for copy in firsts:
        copy.wait()
    inv_root = 1.0 / jnp.sqrt(degree_held[...].astype(jnp.float32)[None, :])
    seeds = seeds_held[...][None, :]
    root_ref[...] = inv_root
    for k, (at, size) in enumerate(chunks(classes)):
        rows = pl.ds(at, size)
        copies[k].wait()
        label = lax.broadcasted_iota(jnp.int32, (size, seeds.shape[1]), 0) + at
        onehot = jnp.where(label == seeds, 1.0, 0.0)
        start = jnp.where(seeds < classes, onehot, held[rows, :].astype(jnp.float32))
        start_ref[rows, :] = start.astype(jnp.bfloat16)
        own_ref[rows, :] = (inv_root * start).astype(jnp.bfloat16)
        put_sends(rows, sends, own_ref, send_refs)


def early_kernel(weight_ref, own_ref, *refs):
    received, sum_ref = refs[:EARLY], refs[EARLY]
    depth = own_ref.shape[1] + EARLY * SIDE
    for at, size in chunks(own_ref.shape[0]):
        rows = pl.ds(at, size)
        sources = jnp.concatenate([own_ref[rows, :]] + [ref[rows, :] for ref in received], axis=1)
        sum_ref[rows, :] = jnp.dot(
            sources, weight_ref[pl.ds(0, depth), :], preferred_element_type=jnp.float32
        )


def new_labels(rows, root_ref, start_ref, weight_ref, sum_ref, received):
    inv_root = root_ref[...]
    depth = len(received) * SIDE
    sources = jnp.concatenate([ref[rows, :] for ref in received], axis=1)
    product = sum_ref[rows, :] + jnp.dot(
        sources,
        weight_ref[pl.ds(weight_ref.shape[0] - depth, depth), :],
        preferred_element_type=jnp.float32,
    )
    labels = 0.9 * inv_root * product + 0.1 * start_ref[rows, :].astype(jnp.float32)
    return inv_root, labels


def step_kernel(send_ref, root_ref, start_ref, weight_ref, sum_ref, *refs):
    late = PERMUTES - EARLY
    received, next_ref, send_refs = refs[:late], refs[late], refs[late + 1 :]
    for at, size in chunks(next_ref.shape[0]):
        rows = pl.ds(at, size)
        inv_root, labels = new_labels(rows, root_ref, start_ref, weight_ref, sum_ref, received)
        next_ref[rows, :] = (inv_root * labels).astype(jnp.bfloat16)
        put_sends(rows, send_ref, next_ref, send_refs)


def last_kernel(root_ref, start_ref, weight_ref, sum_ref, *refs):
    late = PERMUTES - EARLY
    received, (out_ref, held, left) = refs[:late], refs[late:]
    copies = []
    for k, (at, size) in enumerate(chunks(held.shape[0])):
        rows = pl.ds(at, size)
        _, labels = new_labels(rows, root_ref, start_ref, weight_ref, sum_ref, received)
        held[rows, :] = labels
        copies.append(pltpu.make_async_copy(held.at[rows], out_ref.at[rows], left.at[k]))
        copies[-1].start()
    for copy in copies:
        copy.wait()


def weight_kernel(n_group, source_ref, count_ref, tiles_ref, weight_ref, total_ref):
    row_blocks, per_row, side, _ = tiles_ref.shape
    group, core, x = position()
    own = row_blocks
    place = [
        jnp.where(x == 0, own + EDGE, jnp.where(core == 0, own + RING, own + BACK)),
        jnp.where(x == ROW - 1, own + EDGE, jnp.where(core == 0, own + BACK, own + RING)),
        jnp.where(x >= 2, own + TWO, own + CROSS),
        jnp.where(x >= 2, own + CROSS, own + TWO),
        own + UP,
        own + DOWN,
    ]
    for r in range(row_blocks):
        total_ref[...] = jnp.zeros_like(total_ref)
        for t in range(per_row):
            source = source_ref[r, t]
            slot = source
            for k, where in enumerate(place):
                slot = jnp.where(source == own + k, where, slot)
            live = r * per_row + t < count_ref[0]
            live = live & ((source != own + 4) | (group > 0))
            live = live & ((source != own + 5) | (group < n_group - 1))

            @pl.when(live)
            def _():
                total_ref[slot] += tiles_ref[r, t].astype(jnp.float32)

        for s in range(own + PERMUTES):
            weight_ref[pl.ds(s * side, side), pl.ds(r * side, side)] = total_ref[s].T.astype(
                weight_ref.dtype
            )


def on_device(prior, seed_labels, degree, tiles, tile_source, tile_count, send_list):
    row_blocks, _, side, _ = tiles.shape
    nodes, classes = prior.shape
    n_group, n_dom = lax.axis_size("group"), lax.axis_size("dom")
    route = routes(n_group, n_dom)
    slots = row_blocks + PERMUTES
    pieces = len(chunks(classes))
    wide = jax.ShapeDtypeStruct((classes, nodes), jnp.bfloat16)
    narrow = [jax.ShapeDtypeStruct((classes, side), jnp.bfloat16)] * PERMUTES

    inv_root, start, own, *sends = pl.pallas_call(
        prepare_kernel,
        in_specs=[HBM] * 4,
        out_specs=[VMEM] * (3 + PERMUTES),
        out_shape=[jax.ShapeDtypeStruct((1, nodes), jnp.float32), wide, wide] + narrow,
        scratch_shapes=[
            pltpu.SMEM(send_list.shape, jnp.int32),
            pltpu.VMEM((nodes,), jnp.int32),
            pltpu.VMEM((nodes,), jnp.int32),
            pltpu.VMEM((classes, nodes), jnp.bfloat16),
            pltpu.SemaphoreType.DMA((3,)),
            pltpu.SemaphoreType.DMA((pieces,)),
        ],
        compiler_params=PARAMS,
    )(*[in_hbm(x) for x in (send_list, seed_labels, degree, prior.T)])
    weight = pl.pallas_call(
        functools.partial(weight_kernel, n_group),
        in_specs=[SMEM, SMEM, VMEM],
        out_specs=VMEM,
        out_shape=jax.ShapeDtypeStruct((slots * side, nodes), jnp.bfloat16),
        scratch_shapes=[pltpu.VMEM((slots, side, side), jnp.float32)],
        compiler_params=PARAMS,
        cost_estimate=pl.CostEstimate(flops=0, bytes_accessed=8_000_000, transcendentals=0),
    )(tile_source, tile_count, tiles)
    for step in range(ITERS):
        received = [lax.ppermute(sends[k], ("group", "dom"), route[k]) for k in range(PERMUTES)]
        total = pl.pallas_call(
            early_kernel,
            in_specs=[VMEM] * (2 + EARLY),
            out_specs=VMEM,
            out_shape=jax.ShapeDtypeStruct((classes, nodes), jnp.float32),
            compiler_params=PARAMS,
            cost_estimate=pl.CostEstimate(
                flops=2 * classes * nodes * (row_blocks + EARLY) * side,
                bytes_accessed=4_000_000,
                transcendentals=0,
            ),
        )(weight, own, *received[:EARLY])
        late = received[EARLY:]
        if step < ITERS - 1:
            own, *sends = pl.pallas_call(
                step_kernel,
                in_specs=[SMEM] + [VMEM] * (4 + len(late)),
                out_specs=[VMEM] * (1 + PERMUTES),
                out_shape=[wide] + narrow,
                compiler_params=PARAMS,
            )(send_list, inv_root, start, weight, total, *late)
    labels = pl.pallas_call(
        last_kernel,
        in_specs=[VMEM] * (4 + len(late)),
        out_specs=HBM,
        out_shape=jax.ShapeDtypeStruct((classes, nodes), jnp.float32),
        scratch_shapes=[
            pltpu.VMEM((classes, nodes), jnp.float32),
            pltpu.SemaphoreType.DMA((pieces,)),
        ],
        compiler_params=PARAMS,
    )(inv_root, start, weight, total, *late)
    return labels.T


def solution(mesh):
    return jax.shard_map(
        on_device,
        mesh=mesh,
        in_specs=(
            P(("group", "dom"), None),
            P(("group", "dom")),
            P(("group", "dom")),
            P(("group", "dom"), None, None, None),
            P(("group", "dom"), None),
            P(("group", "dom")),
            P(("group", "dom"), None),
        ),
        out_specs=P(("group", "dom"), None),
        check_vma=False,
    )
```

```python
import functools

import jax
import jax.numpy as jnp
from jax import lax
from jax.experimental import pallas as pl
from jax.experimental.pallas import tpu as pltpu
from jax.sharding import PartitionSpec as P

ITERS = 3
CORES = 2
ROW = 4
CHUNK = 256
SIDE = 128
SMEM = pl.BlockSpec(memory_space=pltpu.SMEM)
VMEM = pl.BlockSpec(memory_space=pltpu.VMEM)
HBM = pl.BlockSpec(memory_space=pltpu.HBM)
PARAMS = pltpu.CompilerParams(vmem_limit_bytes=40 * 1024 * 1024)

RING, BACK, TWO, CROSS, EDGE, UP, DOWN = range(7)
PERMUTES = 7
EARLY = 2


def routes(n_group, n_dom):
    def flat(g, d):
        return (g % n_group) * n_dom + d

    places = [(g, d) for g in range(n_group) for d in range(n_dom)]

    def ring(g, d):
        if g % CORES == 0:
            return (g, d + 1) if d % ROW < ROW - 1 else (g + 1, d)
        return (g, d - 1) if d % ROW > 0 else (g - 1, d)

    def pairs(distance, takes):
        both = []
        for g, d in places:
            if takes(d % ROW) and d + distance < n_dom:
                both += [(flat(g, d), flat(g, d + distance)), (flat(g, d + distance), flat(g, d))]
        return both

    forward = [(flat(*p), flat(*ring(*p))) for p in places]
    return {
        RING: forward,
        BACK: [(b, a) for a, b in forward],
        TWO: pairs(2, lambda x: x < 2),
        CROSS: pairs(2, lambda x: x >= 2),
        EDGE: pairs(1, lambda x: x == ROW - 1),
        UP: [(flat(g, d), flat(g + 1, d)) for g, d in places],
        DOWN: [(flat(g, d), flat(g - 1, d)) for g, d in places],
    }


def position():
    group, dom = lax.axis_index("group"), lax.axis_index("dom")
    return group, jnp.bitwise_and(group, CORES - 1), jnp.bitwise_and(dom, ROW - 1)


def columns_to_send():
    _, core, x = position()
    high = x >= 2
    return {
        RING: jnp.where(core == 0, 1, 0),
        BACK: jnp.where(core == 0, 0, 1),
        TWO: jnp.where(high, 2, 3),
        CROSS: jnp.where(high, 3, 2),
        EDGE: jnp.where(x == 0, 0, 1),
        UP: 5,
        DOWN: 4,
    }


def in_hbm(x):
    return pltpu.with_memory_space_constraint(x, pltpu.HBM)


def chunks(rows):
    return [(at, min(CHUNK, rows - at)) for at in range(0, rows, CHUNK)]


def put_sends(rows, send_ref, own_ref, send_refs):
    for k, column in columns_to_send().items():
        block = pl.ds(pl.multiple_of(send_ref[0, column] * SIDE, SIDE), SIDE)
        send_refs[k][rows, :] = own_ref[rows, block]


def prepare_kernel(send_any, seeds_any, degree_any, prior_any, root_ref, start_ref, own_ref, *refs):
    send_refs, (sends, seeds_held, degree_held, held, small, arrived) = refs[:PERMUTES], refs[PERMUTES:]
    classes = prior_any.shape[0]
    firsts = [
        pltpu.make_async_copy(seeds_any, seeds_held, small.at[0]),
        pltpu.make_async_copy(degree_any, degree_held, small.at[1]),
        pltpu.make_async_copy(send_any, sends, small.at[2]),
    ]
    copies = []
    for k, (at, size) in enumerate(chunks(classes)):
        rows = pl.ds(at, size)
        copies.append(pltpu.make_async_copy(prior_any.at[rows], held.at[rows], arrived.at[k]))
    for copy in firsts + copies:
        copy.start()
    for copy in firsts:
        copy.wait()
    inv_root = 1.0 / jnp.sqrt(degree_held[...].astype(jnp.float32)[None, :])
    seeds = seeds_held[...][None, :]
    root_ref[...] = inv_root
    for k, (at, size) in enumerate(chunks(classes)):
        rows = pl.ds(at, size)
        copies[k].wait()
        label = lax.broadcasted_iota(jnp.int32, (size, seeds.shape[1]), 0) + at
        onehot = jnp.where(label == seeds, 1.0, 0.0)
        start = jnp.where(seeds < classes, onehot, held[rows, :].astype(jnp.float32))
        start_ref[rows, :] = start.astype(jnp.bfloat16)
        own_ref[rows, :] = (inv_root * start).astype(jnp.bfloat16)
        put_sends(rows, sends, own_ref, send_refs)


def early_kernel(weight_ref, own_ref, *refs):
    received, sum_ref = refs[:EARLY], refs[EARLY]
    depth = own_ref.shape[1] + EARLY * SIDE
    for at, size in chunks(own_ref.shape[0]):
        rows = pl.ds(at, size)
        sources = jnp.concatenate([own_ref[rows, :]] + [ref[rows, :] for ref in received], axis=1)
        sum_ref[rows, :] = jnp.dot(
            sources, weight_ref[pl.ds(0, depth), :], preferred_element_type=jnp.float32
        )


def new_labels(rows, root_ref, start_ref, weight_ref, sum_ref, received):
    inv_root = root_ref[...]
    depth = len(received) * SIDE
    sources = jnp.concatenate([ref[rows, :] for ref in received], axis=1)
    product = sum_ref[rows, :] + jnp.dot(
        sources,
        weight_ref[pl.ds(weight_ref.shape[0] - depth, depth), :],
        preferred_element_type=jnp.float32,
    )
    labels = 0.9 * inv_root * product + 0.1 * start_ref[rows, :].astype(jnp.float32)
    return inv_root, labels


def step_kernel(send_ref, root_ref, start_ref, weight_ref, sum_ref, *refs):
    late = PERMUTES - EARLY
    received, next_ref, send_refs = refs[:late], refs[late], refs[late + 1 :]
    for at, size in chunks(next_ref.shape[0]):
        rows = pl.ds(at, size)
        inv_root, labels = new_labels(rows, root_ref, start_ref, weight_ref, sum_ref, received)
        next_ref[rows, :] = (inv_root * labels).astype(jnp.bfloat16)
        put_sends(rows, send_ref, next_ref, send_refs)


def last_kernel(root_ref, start_ref, weight_ref, sum_ref, *refs):
    late = PERMUTES - EARLY
    received, (out_ref, held, left) = refs[:late], refs[late:]
    copies = []
    for k, (at, size) in enumerate(chunks(held.shape[0])):
        rows = pl.ds(at, size)
        _, labels = new_labels(rows, root_ref, start_ref, weight_ref, sum_ref, received)
        held[rows, :] = labels
        copies.append(pltpu.make_async_copy(held.at[rows], out_ref.at[rows], left.at[k]))
        copies[-1].start()
    for copy in copies:
        copy.wait()


def weight_kernel(n_group, source_ref, count_ref, tiles_ref, weight_ref, total_ref):
    row_blocks, per_row, side, _ = tiles_ref.shape
    group, core, x = position()
    own = row_blocks
    place = [
        jnp.where(x == 0, own + EDGE, jnp.where(core == 0, own + RING, own + BACK)),
        jnp.where(x == ROW - 1, own + EDGE, jnp.where(core == 0, own + BACK, own + RING)),
        jnp.where(x >= 2, own + TWO, own + CROSS),
        jnp.where(x >= 2, own + CROSS, own + TWO),
        own + UP,
        own + DOWN,
    ]
    for r in range(row_blocks):
        total_ref[...] = jnp.zeros_like(total_ref)
        for t in range(per_row):
            source = source_ref[r, t]
            slot = source
            for k, where in enumerate(place):
                slot = jnp.where(source == own + k, where, slot)
            live = r * per_row + t < count_ref[0]
            live = live & ((source != own + 4) | (group > 0))
            live = live & ((source != own + 5) | (group < n_group - 1))

            @pl.when(live)
            def _():
                total_ref[slot] += tiles_ref[r, t].astype(jnp.float32)

        for s in range(own + PERMUTES):
            weight_ref[pl.ds(s * side, side), pl.ds(r * side, side)] = total_ref[s].T.astype(
                weight_ref.dtype
            )


def on_device(prior, seed_labels, degree, tiles, tile_source, tile_count, send_list):
    row_blocks, _, side, _ = tiles.shape
    nodes, classes = prior.shape
    n_group, n_dom = lax.axis_size("group"), lax.axis_size("dom")
    route = routes(n_group, n_dom)
    slots = row_blocks + PERMUTES
    pieces = len(chunks(classes))
    wide = jax.ShapeDtypeStruct((classes, nodes), jnp.bfloat16)
    narrow = [jax.ShapeDtypeStruct((classes, side), jnp.bfloat16)] * PERMUTES

    inv_root, start, own, *sends = pl.pallas_call(
        prepare_kernel,
        in_specs=[HBM] * 4,
        out_specs=[VMEM] * (3 + PERMUTES),
        out_shape=[jax.ShapeDtypeStruct((1, nodes), jnp.float32), wide, wide] + narrow,
        scratch_shapes=[
            pltpu.SMEM(send_list.shape, jnp.int32),
            pltpu.VMEM((nodes,), jnp.int32),
            pltpu.VMEM((nodes,), jnp.int32),
            pltpu.VMEM((classes, nodes), jnp.bfloat16),
            pltpu.SemaphoreType.DMA((3,)),
            pltpu.SemaphoreType.DMA((pieces,)),
        ],
        compiler_params=PARAMS,
    )(*[in_hbm(x) for x in (send_list, seed_labels, degree, prior.T)])
    weight = pl.pallas_call(
        functools.partial(weight_kernel, n_group),
        in_specs=[SMEM, SMEM, VMEM],
        out_specs=VMEM,
        out_shape=jax.ShapeDtypeStruct((slots * side, nodes), jnp.bfloat16),
        scratch_shapes=[pltpu.VMEM((slots, side, side), jnp.float32)],
        compiler_params=PARAMS,
        cost_estimate=pl.CostEstimate(flops=0, bytes_accessed=8_000_000, transcendentals=0),
    )(tile_source, tile_count, tiles)
    for step in range(ITERS):
        received = [lax.ppermute(sends[k], ("group", "dom"), route[k]) for k in range(PERMUTES)]
        total = pl.pallas_call(
            early_kernel,
            in_specs=[VMEM] * (2 + EARLY),
            out_specs=VMEM,
            out_shape=jax.ShapeDtypeStruct((classes, nodes), jnp.float32),
            compiler_params=PARAMS,
            cost_estimate=pl.CostEstimate(
                flops=2 * classes * nodes * (row_blocks + EARLY) * side,
                bytes_accessed=4_000_000,
                transcendentals=0,
            ),
        )(weight, own, *received[:EARLY])
        late = received[EARLY:]
        if step < ITERS - 1:
            own, *sends = pl.pallas_call(
                step_kernel,
                in_specs=[SMEM] + [VMEM] * (4 + len(late)),
                out_specs=[VMEM] * (1 + PERMUTES),
                out_shape=[wide] + narrow,
                compiler_params=PARAMS,
            )(send_list, inv_root, start, weight, total, *late)
    labels = pl.pallas_call(
        last_kernel,
        in_specs=[VMEM] * (4 + len(late)),
        out_specs=HBM,
        out_shape=jax.ShapeDtypeStruct((classes, nodes), jnp.float32),
        scratch_shapes=[
            pltpu.VMEM((classes, nodes), jnp.float32),
            pltpu.SemaphoreType.DMA((pieces,)),
        ],
        compiler_params=PARAMS,
    )(inv_root, start, weight, total, *late)
    return labels.T


def solution(mesh):
    return jax.shard_map(
        on_device,
        mesh=mesh,
        in_specs=(
            P(("group", "dom"), None),
            P(("group", "dom")),
            P(("group", "dom")),
            P(("group", "dom"), None, None, None),
            P(("group", "dom"), None),
            P(("group", "dom")),
            P(("group", "dom"), None),
        ),
        out_specs=P(("group", "dom"), None),
        check_vma=False,
    )
```

```python
import functools

import jax
import jax.numpy as jnp
from jax import lax
from jax.experimental import pallas as pl
from jax.experimental.pallas import tpu as pltpu
from jax.sharding import PartitionSpec as P

ITERS = 3
CORES = 2
ROW = 4
CHUNK = 256
SIDE = 128
SMEM = pl.BlockSpec(memory_space=pltpu.SMEM)
VMEM = pl.BlockSpec(memory_space=pltpu.VMEM)
HBM = pl.BlockSpec(memory_space=pltpu.HBM)
PARAMS = pltpu.CompilerParams(vmem_limit_bytes=40 * 1024 * 1024)

EDGE, RING, BACK, TWO, CROSS, UP, DOWN = range(7)
PERMUTES = 7
EARLY = 3


def routes(n_group, n_dom):
    def flat(g, d):
        return (g % n_group) * n_dom + d

    places = [(g, d) for g in range(n_group) for d in range(n_dom)]

    def ring(g, d):
        if g % CORES == 0:
            return (g, d + 1) if d % ROW < ROW - 1 else (g + 1, d)
        return (g, d - 1) if d % ROW > 0 else (g - 1, d)

    def pairs(distance, takes):
        both = []
        for g, d in places:
            if takes(d % ROW) and d + distance < n_dom:
                both += [(flat(g, d), flat(g, d + distance)), (flat(g, d + distance), flat(g, d))]
        return both

    forward = [(flat(*p), flat(*ring(*p))) for p in places]
    return {
        RING: forward,
        BACK: [(b, a) for a, b in forward],
        TWO: pairs(2, lambda x: x < 2),
        CROSS: pairs(2, lambda x: x >= 2),
        EDGE: pairs(1, lambda x: x == ROW - 1),
        UP: [(flat(g, d), flat(g + 1, d)) for g, d in places],
        DOWN: [(flat(g, d), flat(g - 1, d)) for g, d in places],
    }


def position():
    group, dom = lax.axis_index("group"), lax.axis_index("dom")
    return group, jnp.bitwise_and(group, CORES - 1), jnp.bitwise_and(dom, ROW - 1)


def columns_to_send():
    _, core, x = position()
    high = x >= 2
    return {
        RING: jnp.where(core == 0, 1, 0),
        BACK: jnp.where(core == 0, 0, 1),
        TWO: jnp.where(high, 2, 3),
        CROSS: jnp.where(high, 3, 2),
        EDGE: jnp.where(x == 0, 0, 1),
        UP: 5,
        DOWN: 4,
    }


def in_hbm(x):
    return pltpu.with_memory_space_constraint(x, pltpu.HBM)


def chunks(rows):
    return [(at, min(CHUNK, rows - at)) for at in range(0, rows, CHUNK)]


def put_sends(rows, send_ref, own_ref, send_refs):
    for k, column in columns_to_send().items():
        block = pl.ds(pl.multiple_of(send_ref[0, column] * SIDE, SIDE), SIDE)
        send_refs[k][rows, :] = own_ref[rows, block]


def prepare_kernel(send_any, seeds_any, degree_any, prior_any, root_ref, start_ref, own_ref, *refs):
    send_refs, (sends, seeds_held, degree_held, held, small, arrived) = refs[:PERMUTES], refs[PERMUTES:]
    classes = prior_any.shape[0]
    firsts = [
        pltpu.make_async_copy(seeds_any, seeds_held, small.at[0]),
        pltpu.make_async_copy(degree_any, degree_held, small.at[1]),
        pltpu.make_async_copy(send_any, sends, small.at[2]),
    ]
    copies = []
    for k, (at, size) in enumerate(chunks(classes)):
        rows = pl.ds(at, size)
        copies.append(pltpu.make_async_copy(prior_any.at[rows], held.at[rows], arrived.at[k]))
    for copy in firsts + copies:
        copy.start()
    for copy in firsts:
        copy.wait()
    inv_root = 1.0 / jnp.sqrt(degree_held[...].astype(jnp.float32)[None, :])
    seeds = seeds_held[...][None, :]
    root_ref[...] = inv_root
    for k, (at, size) in enumerate(chunks(classes)):
        rows = pl.ds(at, size)
        copies[k].wait()
        label = lax.broadcasted_iota(jnp.int32, (size, seeds.shape[1]), 0) + at
        onehot = jnp.where(label == seeds, 1.0, 0.0)
        start = jnp.where(seeds < classes, onehot, held[rows, :].astype(jnp.float32))
        start_ref[rows, :] = start.astype(jnp.bfloat16)
        own_ref[rows, :] = (inv_root * start).astype(jnp.bfloat16)
        put_sends(rows, sends, own_ref, send_refs)


def early_kernel(weight_ref, own_ref, *refs):
    received, sum_ref = refs[:EARLY], refs[EARLY]
    depth = own_ref.shape[1] + EARLY * SIDE
    for at, size in chunks(own_ref.shape[0]):
        rows = pl.ds(at, size)
        sources = jnp.concatenate([own_ref[rows, :]] + [ref[rows, :] for ref in received], axis=1)
        sum_ref[rows, :] = jnp.dot(
            sources, weight_ref[pl.ds(0, depth), :], preferred_element_type=jnp.float32
        )


def new_labels(rows, root_ref, start_ref, weight_ref, sum_ref, received):
    inv_root = root_ref[...]
    depth = len(received) * SIDE
    sources = jnp.concatenate([ref[rows, :] for ref in received], axis=1)
    product = sum_ref[rows, :] + jnp.dot(
        sources,
        weight_ref[pl.ds(weight_ref.shape[0] - depth, depth), :],
        preferred_element_type=jnp.float32,
    )
    labels = 0.9 * inv_root * product + 0.1 * start_ref[rows, :].astype(jnp.float32)
    return inv_root, labels


def step_kernel(send_ref, root_ref, start_ref, weight_ref, sum_ref, *refs):
    late = PERMUTES - EARLY
    received, next_ref, send_refs = refs[:late], refs[late], refs[late + 1 :]
    for at, size in chunks(next_ref.shape[0]):
        rows = pl.ds(at, size)
        inv_root, labels = new_labels(rows, root_ref, start_ref, weight_ref, sum_ref, received)
        next_ref[rows, :] = (inv_root * labels).astype(jnp.bfloat16)
        put_sends(rows, send_ref, next_ref, send_refs)


def last_kernel(root_ref, start_ref, weight_ref, sum_ref, *refs):
    late = PERMUTES - EARLY
    received, (out_ref, held, left) = refs[:late], refs[late:]
    copies = []
    for k, (at, size) in enumerate(chunks(held.shape[0])):
        rows = pl.ds(at, size)
        _, labels = new_labels(rows, root_ref, start_ref, weight_ref, sum_ref, received)
        held[rows, :] = labels
        copies.append(pltpu.make_async_copy(held.at[rows], out_ref.at[rows], left.at[k]))
        copies[-1].start()
    for copy in copies:
        copy.wait()


def weight_kernel(n_group, source_ref, count_ref, tiles_ref, weight_ref, total_ref):
    row_blocks, per_row, side, _ = tiles_ref.shape
    group, core, x = position()
    own = row_blocks
    place = [
        jnp.where(x == 0, own + EDGE, jnp.where(core == 0, own + RING, own + BACK)),
        jnp.where(x == ROW - 1, own + EDGE, jnp.where(core == 0, own + BACK, own + RING)),
        jnp.where(x >= 2, own + TWO, own + CROSS),
        jnp.where(x >= 2, own + CROSS, own + TWO),
        own + UP,
        own + DOWN,
    ]
    for r in range(row_blocks):
        total_ref[...] = jnp.zeros_like(total_ref)
        for t in range(per_row):
            source = source_ref[r, t]
            slot = source
            for k, where in enumerate(place):
                slot = jnp.where(source == own + k, where, slot)
            live = r * per_row + t < count_ref[0]
            live = live & ((source != own + 4) | (group > 0))
            live = live & ((source != own + 5) | (group < n_group - 1))

            @pl.when(live)
            def _():
                total_ref[slot] += tiles_ref[r, t].astype(jnp.float32)

        for s in range(own + PERMUTES):
            weight_ref[pl.ds(s * side, side), pl.ds(r * side, side)] = total_ref[s].T.astype(
                weight_ref.dtype
            )


def on_device(prior, seed_labels, degree, tiles, tile_source, tile_count, send_list):
    row_blocks, _, side, _ = tiles.shape
    nodes, classes = prior.shape
    n_group, n_dom = lax.axis_size("group"), lax.axis_size("dom")
    route = routes(n_group, n_dom)
    slots = row_blocks + PERMUTES
    pieces = len(chunks(classes))
    wide = jax.ShapeDtypeStruct((classes, nodes), jnp.bfloat16)
    narrow = [jax.ShapeDtypeStruct((classes, side), jnp.bfloat16)] * PERMUTES

    inv_root, start, own, *sends = pl.pallas_call(
        prepare_kernel,
        in_specs=[HBM] * 4,
        out_specs=[VMEM] * (3 + PERMUTES),
        out_shape=[jax.ShapeDtypeStruct((1, nodes), jnp.float32), wide, wide] + narrow,
        scratch_shapes=[
            pltpu.SMEM(send_list.shape, jnp.int32),
            pltpu.VMEM((nodes,), jnp.int32),
            pltpu.VMEM((nodes,), jnp.int32),
            pltpu.VMEM((classes, nodes), jnp.bfloat16),
            pltpu.SemaphoreType.DMA((3,)),
            pltpu.SemaphoreType.DMA((pieces,)),
        ],
        compiler_params=PARAMS,
    )(*[in_hbm(x) for x in (send_list, seed_labels, degree, prior.T)])
    weight = pl.pallas_call(
        functools.partial(weight_kernel, n_group),
        in_specs=[SMEM, SMEM, VMEM],
        out_specs=VMEM,
        out_shape=jax.ShapeDtypeStruct((slots * side, nodes), jnp.bfloat16),
        scratch_shapes=[pltpu.VMEM((slots, side, side), jnp.float32)],
        compiler_params=PARAMS,
        cost_estimate=pl.CostEstimate(flops=0, bytes_accessed=8_000_000, transcendentals=0),
    )(tile_source, tile_count, tiles)
    for step in range(ITERS):
        received = [lax.ppermute(sends[k], ("group", "dom"), route[k]) for k in range(PERMUTES)]
        total = pl.pallas_call(
            early_kernel,
            in_specs=[VMEM] * (2 + EARLY),
            out_specs=VMEM,
            out_shape=jax.ShapeDtypeStruct((classes, nodes), jnp.float32),
            compiler_params=PARAMS,
            cost_estimate=pl.CostEstimate(
                flops=2 * classes * nodes * (row_blocks + EARLY) * side,
                bytes_accessed=4_000_000,
                transcendentals=0,
            ),
        )(weight, own, *received[:EARLY])
        late = received[EARLY:]
        if step < ITERS - 1:
            own, *sends = pl.pallas_call(
                step_kernel,
                in_specs=[SMEM] + [VMEM] * (4 + len(late)),
                out_specs=[VMEM] * (1 + PERMUTES),
                out_shape=[wide] + narrow,
                compiler_params=PARAMS,
            )(send_list, inv_root, start, weight, total, *late)
    labels = pl.pallas_call(
        last_kernel,
        in_specs=[VMEM] * (4 + len(late)),
        out_specs=HBM,
        out_shape=jax.ShapeDtypeStruct((classes, nodes), jnp.float32),
        scratch_shapes=[
            pltpu.VMEM((classes, nodes), jnp.float32),
            pltpu.SemaphoreType.DMA((pieces,)),
        ],
        compiler_params=PARAMS,
    )(inv_root, start, weight, total, *late)
    return labels.T


def solution(mesh):
    return jax.shard_map(
        on_device,
        mesh=mesh,
        in_specs=(
            P(("group", "dom"), None),
            P(("group", "dom")),
            P(("group", "dom")),
            P(("group", "dom"), None, None, None),
            P(("group", "dom"), None),
            P(("group", "dom")),
            P(("group", "dom"), None),
        ),
        out_specs=P(("group", "dom"), None),
        check_vma=False,
    )
```

```python
import functools

import jax
import jax.numpy as jnp
from jax import lax
from jax.experimental import pallas as pl
from jax.experimental.pallas import tpu as pltpu
from jax.sharding import PartitionSpec as P

ITERS = 3
CORES = 2
ROW = 4
CHUNK = 256
SIDE = 128
SMEM = pl.BlockSpec(memory_space=pltpu.SMEM)
VMEM = pl.BlockSpec(memory_space=pltpu.VMEM)
HBM = pl.BlockSpec(memory_space=pltpu.HBM)
PARAMS = pltpu.CompilerParams(vmem_limit_bytes=40 * 1024 * 1024)

EDGE, RING, BACK, TWO, CROSS, UP, DOWN = range(7)
PERMUTES = 7
EARLY = 3


def routes(n_group, n_dom):
    def flat(g, d):
        return (g % n_group) * n_dom + d

    places = [(g, d) for g in range(n_group) for d in range(n_dom)]

    def ring(g, d):
        if g % CORES == 0:
            return (g, d + 1) if d % ROW < ROW - 1 else (g + 1, d)
        return (g, d - 1) if d % ROW > 0 else (g - 1, d)

    def pairs(distance, takes):
        both = []
        for g, d in places:
            if takes(d % ROW) and d + distance < n_dom:
                both += [(flat(g, d), flat(g, d + distance)), (flat(g, d + distance), flat(g, d))]
        return both

    forward = [(flat(*p), flat(*ring(*p))) for p in places]
    return {
        RING: forward,
        BACK: [(b, a) for a, b in forward],
        TWO: pairs(2, lambda x: x < 2),
        CROSS: pairs(2, lambda x: x >= 2),
        EDGE: pairs(1, lambda x: x == ROW - 1),
        UP: [(flat(g, d), flat(g + 1, d)) for g, d in places],
        DOWN: [(flat(g, d), flat(g - 1, d)) for g, d in places],
    }


def position():
    group, dom = lax.axis_index("group"), lax.axis_index("dom")
    return group, jnp.bitwise_and(group, CORES - 1), jnp.bitwise_and(dom, ROW - 1)


def columns_to_send():
    _, core, x = position()
    high = x >= 2
    return {
        RING: jnp.where(core == 0, 1, 0),
        BACK: jnp.where(core == 0, 0, 1),
        TWO: jnp.where(high, 2, 3),
        CROSS: jnp.where(high, 3, 2),
        EDGE: jnp.where(x == 0, 0, 1),
        UP: 5,
        DOWN: 4,
    }


def in_hbm(x):
    return pltpu.with_memory_space_constraint(x, pltpu.HBM)


def chunks(rows):
    return [(at, min(CHUNK, rows - at)) for at in range(0, rows, CHUNK)]


def put_sends(rows, send_ref, own_ref, send_refs):
    for k, column in columns_to_send().items():
        block = pl.ds(pl.multiple_of(send_ref[0, column] * SIDE, SIDE), SIDE)
        send_refs[k][rows, :] = own_ref[rows, block]


def prepare_kernel(send_any, seeds_any, degree_any, prior_any, root_ref, start_ref, own_ref, *refs):
    send_refs, (sends, seeds_held, degree_held, held, small, arrived) = refs[:PERMUTES], refs[PERMUTES:]
    classes = prior_any.shape[0]
    firsts = [
        pltpu.make_async_copy(seeds_any, seeds_held, small.at[0]),
        pltpu.make_async_copy(degree_any, degree_held, small.at[1]),
        pltpu.make_async_copy(send_any, sends, small.at[2]),
    ]
    copies = []
    for k, (at, size) in enumerate(chunks(classes)):
        rows = pl.ds(at, size)
        copies.append(pltpu.make_async_copy(prior_any.at[rows], held.at[rows], arrived.at[k]))
    for copy in firsts + copies:
        copy.start()
    for copy in firsts:
        copy.wait()
    inv_root = 1.0 / jnp.sqrt(degree_held[...].astype(jnp.float32)[None, :])
    seeds = seeds_held[...][None, :]
    root_ref[...] = inv_root
    for k, (at, size) in enumerate(chunks(classes)):
        rows = pl.ds(at, size)
        copies[k].wait()
        label = lax.broadcasted_iota(jnp.int32, (size, seeds.shape[1]), 0) + at
        onehot = jnp.where(label == seeds, 1.0, 0.0)
        start = jnp.where(seeds < classes, onehot, held[rows, :].astype(jnp.float32))
        start_ref[rows, :] = start.astype(jnp.bfloat16)
        own_ref[rows, :] = (inv_root * start).astype(jnp.bfloat16)
        put_sends(rows, sends, own_ref, send_refs)


def gains(root_ref, last):
    inv_root = root_ref[...]
    if last:
        return 0.9 * inv_root, 0.1
    return inv_root * (0.9 * inv_root), 0.1 * inv_root


def early_kernel(last, root_ref, start_ref, weight_ref, own_ref, *refs):
    received, sum_ref = refs[:EARLY], refs[EARLY]
    depth = own_ref.shape[1] + EARLY * SIDE
    of_product, of_start = gains(root_ref, last)
    for at, size in chunks(own_ref.shape[0]):
        rows = pl.ds(at, size)
        sources = jnp.concatenate([own_ref[rows, :]] + [ref[rows, :] for ref in received], axis=1)
        product = jnp.dot(
            sources, weight_ref[pl.ds(0, depth), :], preferred_element_type=jnp.float32
        )
        start = start_ref[rows, :].astype(jnp.float32)
        sum_ref[rows, :] = of_product * product + of_start * start


def finished(last, rows, root_ref, weight_ref, sum_ref, received):
    depth = len(received) * SIDE
    product = jnp.dot(
        jnp.concatenate([ref[rows, :] for ref in received], axis=1),
        weight_ref[pl.ds(weight_ref.shape[0] - depth, depth), :],
        preferred_element_type=jnp.float32,
    )
    return sum_ref[rows, :] + gains(root_ref, last)[0] * product


def step_kernel(send_ref, root_ref, weight_ref, sum_ref, *refs):
    late = PERMUTES - EARLY
    received, next_ref, send_refs = refs[:late], refs[late], refs[late + 1 :]
    for at, size in chunks(next_ref.shape[0]):
        rows = pl.ds(at, size)
        scaled = finished(False, rows, root_ref, weight_ref, sum_ref, received)
        next_ref[rows, :] = scaled.astype(jnp.bfloat16)
        put_sends(rows, send_ref, next_ref, send_refs)


def last_kernel(root_ref, weight_ref, sum_ref, *refs):
    late = PERMUTES - EARLY
    received, (out_ref, held, left) = refs[:late], refs[late:]
    copies = []
    for k, (at, size) in enumerate(chunks(held.shape[0])):
        rows = pl.ds(at, size)
        held[rows, :] = finished(True, rows, root_ref, weight_ref, sum_ref, received)
        copies.append(pltpu.make_async_copy(held.at[rows], out_ref.at[rows], left.at[k]))
        copies[-1].start()
    for copy in copies:
        copy.wait()


def weight_kernel(n_group, source_ref, count_ref, tiles_ref, weight_ref, total_ref):
    row_blocks, per_row, side, _ = tiles_ref.shape
    group, core, x = position()
    own = row_blocks
    place = [
        jnp.where(x == 0, own + EDGE, jnp.where(core == 0, own + RING, own + BACK)),
        jnp.where(x == ROW - 1, own + EDGE, jnp.where(core == 0, own + BACK, own + RING)),
        jnp.where(x >= 2, own + TWO, own + CROSS),
        jnp.where(x >= 2, own + CROSS, own + TWO),
        own + UP,
        own + DOWN,
    ]
    for r in range(row_blocks):
        total_ref[...] = jnp.zeros_like(total_ref)
        for t in range(per_row):
            source = source_ref[r, t]
            slot = source
            for k, where in enumerate(place):
                slot = jnp.where(source == own + k, where, slot)
            live = r * per_row + t < count_ref[0]
            live = live & ((source != own + 4) | (group > 0))
            live = live & ((source != own + 5) | (group < n_group - 1))

            @pl.when(live)
            def _():
                total_ref[slot] += tiles_ref[r, t].astype(jnp.float32)

        for s in range(own + PERMUTES):
            weight_ref[pl.ds(s * side, side), pl.ds(r * side, side)] = total_ref[s].T.astype(
                weight_ref.dtype
            )


def on_device(prior, seed_labels, degree, tiles, tile_source, tile_count, send_list):
    row_blocks, _, side, _ = tiles.shape
    nodes, classes = prior.shape
    n_group, n_dom = lax.axis_size("group"), lax.axis_size("dom")
    route = routes(n_group, n_dom)
    slots = row_blocks + PERMUTES
    pieces = len(chunks(classes))
    wide = jax.ShapeDtypeStruct((classes, nodes), jnp.bfloat16)
    narrow = [jax.ShapeDtypeStruct((classes, side), jnp.bfloat16)] * PERMUTES

    inv_root, start, own, *sends = pl.pallas_call(
        prepare_kernel,
        in_specs=[HBM] * 4,
        out_specs=[VMEM] * (3 + PERMUTES),
        out_shape=[jax.ShapeDtypeStruct((1, nodes), jnp.float32), wide, wide] + narrow,
        scratch_shapes=[
            pltpu.SMEM(send_list.shape, jnp.int32),
            pltpu.VMEM((nodes,), jnp.int32),
            pltpu.VMEM((nodes,), jnp.int32),
            pltpu.VMEM((classes, nodes), jnp.bfloat16),
            pltpu.SemaphoreType.DMA((3,)),
            pltpu.SemaphoreType.DMA((pieces,)),
        ],
        compiler_params=PARAMS,
    )(*[in_hbm(x) for x in (send_list, seed_labels, degree, prior.T)])
    weight = pl.pallas_call(
        functools.partial(weight_kernel, n_group),
        in_specs=[SMEM, SMEM, VMEM],
        out_specs=VMEM,
        out_shape=jax.ShapeDtypeStruct((slots * side, nodes), jnp.bfloat16),
        scratch_shapes=[pltpu.VMEM((slots, side, side), jnp.float32)],
        compiler_params=PARAMS,
        cost_estimate=pl.CostEstimate(flops=0, bytes_accessed=8_000_000, transcendentals=0),
    )(tile_source, tile_count, tiles)
    for step in range(ITERS):
        received = [lax.ppermute(sends[k], ("group", "dom"), route[k]) for k in range(PERMUTES)]
        total = pl.pallas_call(
            functools.partial(early_kernel, step == ITERS - 1),
            in_specs=[VMEM] * (4 + EARLY),
            out_specs=VMEM,
            out_shape=jax.ShapeDtypeStruct((classes, nodes), jnp.float32),
            compiler_params=PARAMS,
            cost_estimate=pl.CostEstimate(
                flops=2 * classes * nodes * (row_blocks + EARLY) * side,
                bytes_accessed=4_000_000,
                transcendentals=0,
            ),
        )(inv_root, start, weight, own, *received[:EARLY])
        late = received[EARLY:]
        if step < ITERS - 1:
            own, *sends = pl.pallas_call(
                step_kernel,
                in_specs=[SMEM] + [VMEM] * (3 + len(late)),
                out_specs=[VMEM] * (1 + PERMUTES),
                out_shape=[wide] + narrow,
                compiler_params=PARAMS,
            )(send_list, inv_root, weight, total, *late)
    labels = pl.pallas_call(
        last_kernel,
        in_specs=[VMEM] * (3 + len(late)),
        out_specs=HBM,
        out_shape=jax.ShapeDtypeStruct((classes, nodes), jnp.float32),
        scratch_shapes=[
            pltpu.VMEM((classes, nodes), jnp.float32),
            pltpu.SemaphoreType.DMA((pieces,)),
        ],
        compiler_params=PARAMS,
    )(inv_root, weight, total, *late)
    return labels.T


def solution(mesh):
    return jax.shard_map(
        on_device,
        mesh=mesh,
        in_specs=(
            P(("group", "dom"), None),
            P(("group", "dom")),
            P(("group", "dom")),
            P(("group", "dom"), None, None, None),
            P(("group", "dom"), None),
            P(("group", "dom")),
            P(("group", "dom"), None),
        ),
        out_specs=P(("group", "dom"), None),
        check_vma=False,
    )
```

```python
import functools

import jax
import jax.numpy as jnp
from jax import lax
from jax.experimental import pallas as pl
from jax.experimental.pallas import tpu as pltpu
from jax.sharding import PartitionSpec as P

ITERS = 3
CORES = 2
ROW = 4
CHUNK = 256
SIDE = 128
SMEM = pl.BlockSpec(memory_space=pltpu.SMEM)
VMEM = pl.BlockSpec(memory_space=pltpu.VMEM)
HBM = pl.BlockSpec(memory_space=pltpu.HBM)
PARAMS = pltpu.CompilerParams(vmem_limit_bytes=40 * 1024 * 1024)

RING, EDGE, BACK, TWO, CROSS, UP, DOWN = range(7)
PERMUTES = 7
EARLY = 3


def routes(n_group, n_dom):
    def flat(g, d):
        return (g % n_group) * n_dom + d

    places = [(g, d) for g in range(n_group) for d in range(n_dom)]

    def ring(g, d):
        if g % CORES == 0:
            return (g, d + 1) if d % ROW < ROW - 1 else (g + 1, d)
        return (g, d - 1) if d % ROW > 0 else (g - 1, d)

    def pairs(distance, takes):
        both = []
        for g, d in places:
            if takes(d % ROW) and d + distance < n_dom:
                both += [(flat(g, d), flat(g, d + distance)), (flat(g, d + distance), flat(g, d))]
        return both

    forward = [(flat(*p), flat(*ring(*p))) for p in places]
    return {
        RING: forward,
        BACK: [(b, a) for a, b in forward],
        TWO: pairs(2, lambda x: x < 2),
        CROSS: pairs(2, lambda x: x >= 2),
        EDGE: pairs(1, lambda x: x == ROW - 1),
        UP: [(flat(g, d), flat(g + 1, d)) for g, d in places],
        DOWN: [(flat(g, d), flat(g - 1, d)) for g, d in places],
    }


def position():
    group, dom = lax.axis_index("group"), lax.axis_index("dom")
    return group, jnp.bitwise_and(group, CORES - 1), jnp.bitwise_and(dom, ROW - 1)


def columns_to_send():
    _, core, x = position()
    high = x >= 2
    return {
        RING: jnp.where(core == 0, 1, 0),
        BACK: jnp.where(core == 0, 0, 1),
        TWO: jnp.where(high, 2, 3),
        CROSS: jnp.where(high, 3, 2),
        EDGE: jnp.where(x == 0, 0, 1),
        UP: 5,
        DOWN: 4,
    }


def in_hbm(x):
    return pltpu.with_memory_space_constraint(x, pltpu.HBM)


def chunks(rows):
    return [(at, min(CHUNK, rows - at)) for at in range(0, rows, CHUNK)]


def put_sends(rows, send_ref, own_ref, send_refs):
    for k, column in columns_to_send().items():
        block = pl.ds(pl.multiple_of(send_ref[0, column] * SIDE, SIDE), SIDE)
        send_refs[k][rows, :] = own_ref[rows, block]


def start_of(rows, at, classes, seeds, prior_ref):
    soft = prior_ref[rows, :].astype(jnp.float32)
    label = lax.broadcasted_iota(jnp.int32, soft.shape, 0) + at
    return jnp.where(seeds < classes, jnp.where(label == seeds, 1.0, 0.0), soft)


def prepare_kernel(
    send_any, seeds_any, degree_any, prior_any, root_ref, seeds_ref, prior_ref, own_ref, *refs
):
    send_refs, (sends, seeds_held, degree_held, arrived) = refs[:PERMUTES], refs[PERMUTES:]
    classes = prior_any.shape[0]
    copies = [
        pltpu.make_async_copy(prior_any, prior_ref, arrived.at[0]),
        pltpu.make_async_copy(seeds_any, seeds_held, arrived.at[1]),
        pltpu.make_async_copy(degree_any, degree_held, arrived.at[2]),
        pltpu.make_async_copy(send_any, sends, arrived.at[3]),
    ]
    for copy in copies:
        copy.start()
    for copy in copies:
        copy.wait()
    inv_root = 1.0 / jnp.sqrt(degree_held[...].astype(jnp.float32)[None, :])
    seeds = seeds_held[...][None, :]
    root_ref[...] = inv_root
    seeds_ref[...] = seeds
    for at, size in chunks(classes):
        rows = pl.ds(at, size)
        start = start_of(rows, at, classes, seeds, prior_ref)
        own_ref[rows, :] = (inv_root * start).astype(jnp.bfloat16)
        put_sends(rows, sends, own_ref, send_refs)


def gains(root_ref, last):
    inv_root = root_ref[...]
    if last:
        return 0.9 * inv_root, 0.1
    return inv_root * (0.9 * inv_root), 0.1 * inv_root


def early_kernel(last, root_ref, seeds_ref, prior_ref, weight_ref, own_ref, *refs):
    received, sum_ref = refs[:EARLY], refs[EARLY]
    depth = own_ref.shape[1] + EARLY * SIDE
    of_product, of_start = gains(root_ref, last)
    for at, size in chunks(own_ref.shape[0]):
        rows = pl.ds(at, size)
        sources = jnp.concatenate([own_ref[rows, :]] + [ref[rows, :] for ref in received], axis=1)
        product = jnp.dot(
            sources, weight_ref[pl.ds(0, depth), :], preferred_element_type=jnp.float32
        )
        start = start_of(rows, at, prior_ref.shape[0], seeds_ref[...], prior_ref)
        sum_ref[rows, :] = of_product * product + of_start * start


def finished(last, rows, root_ref, weight_ref, sum_ref, received):
    depth = len(received) * SIDE
    product = jnp.dot(
        jnp.concatenate([ref[rows, :] for ref in received], axis=1),
        weight_ref[pl.ds(weight_ref.shape[0] - depth, depth), :],
        preferred_element_type=jnp.float32,
    )
    return sum_ref[rows, :] + gains(root_ref, last)[0] * product


def step_kernel(send_ref, root_ref, weight_ref, sum_ref, *refs):
    late = PERMUTES - EARLY
    received, next_ref, send_refs = refs[:late], refs[late], refs[late + 1 :]
    for at, size in chunks(next_ref.shape[0]):
        rows = pl.ds(at, size)
        scaled = finished(False, rows, root_ref, weight_ref, sum_ref, received)
        next_ref[rows, :] = scaled.astype(jnp.bfloat16)
        put_sends(rows, send_ref, next_ref, send_refs)


def last_kernel(root_ref, weight_ref, sum_ref, *refs):
    late = PERMUTES - EARLY
    received, (out_ref, held, left) = refs[:late], refs[late:]
    copies = []
    for k, (at, size) in enumerate(chunks(held.shape[0])):
        rows = pl.ds(at, size)
        held[rows, :] = finished(True, rows, root_ref, weight_ref, sum_ref, received)
        copies.append(pltpu.make_async_copy(held.at[rows], out_ref.at[rows], left.at[k]))
        copies[-1].start()
    for copy in copies:
        copy.wait()


def weight_kernel(n_group, source_ref, count_ref, tiles_ref, weight_ref, total_ref):
    row_blocks, per_row, side, _ = tiles_ref.shape
    group, core, x = position()
    own = row_blocks
    place = [
        jnp.where(x == 0, own + EDGE, jnp.where(core == 0, own + RING, own + BACK)),
        jnp.where(x == ROW - 1, own + EDGE, jnp.where(core == 0, own + BACK, own + RING)),
        jnp.where(x >= 2, own + TWO, own + CROSS),
        jnp.where(x >= 2, own + CROSS, own + TWO),
        own + UP,
        own + DOWN,
    ]
    for r in range(row_blocks):
        total_ref[...] = jnp.zeros_like(total_ref)
        for t in range(per_row):
            source = source_ref[r, t]
            slot = source
            for k, where in enumerate(place):
                slot = jnp.where(source == own + k, where, slot)
            live = r * per_row + t < count_ref[0]
            live = live & ((source != own + 4) | (group > 0))
            live = live & ((source != own + 5) | (group < n_group - 1))

            @pl.when(live)
            def _():
                total_ref[slot] += tiles_ref[r, t].astype(jnp.float32)

        for s in range(own + PERMUTES):
            weight_ref[pl.ds(s * side, side), pl.ds(r * side, side)] = total_ref[s].T.astype(
                weight_ref.dtype
            )


def on_device(prior, seed_labels, degree, tiles, tile_source, tile_count, send_list):
    row_blocks, _, side, _ = tiles.shape
    nodes, classes = prior.shape
    n_group, n_dom = lax.axis_size("group"), lax.axis_size("dom")
    route = routes(n_group, n_dom)
    slots = row_blocks + PERMUTES
    pieces = len(chunks(classes))
    wide = jax.ShapeDtypeStruct((classes, nodes), jnp.bfloat16)
    narrow = [jax.ShapeDtypeStruct((classes, side), jnp.bfloat16)] * PERMUTES

    inv_root, seeds, soft, own, *sends = pl.pallas_call(
        prepare_kernel,
        in_specs=[HBM] * 4,
        out_specs=[VMEM] * (4 + PERMUTES),
        out_shape=[
            jax.ShapeDtypeStruct((1, nodes), jnp.float32),
            jax.ShapeDtypeStruct((1, nodes), jnp.int32),
            wide,
            wide,
        ]
        + narrow,
        scratch_shapes=[
            pltpu.SMEM(send_list.shape, jnp.int32),
            pltpu.VMEM((nodes,), jnp.int32),
            pltpu.VMEM((nodes,), jnp.int32),
            pltpu.SemaphoreType.DMA((4,)),
        ],
        compiler_params=PARAMS,
    )(*[in_hbm(x) for x in (send_list, seed_labels, degree, prior.T)])
    weight = pl.pallas_call(
        functools.partial(weight_kernel, n_group),
        in_specs=[SMEM, SMEM, VMEM],
        out_specs=VMEM,
        out_shape=jax.ShapeDtypeStruct((slots * side, nodes), jnp.bfloat16),
        scratch_shapes=[pltpu.VMEM((slots, side, side), jnp.float32)],
        compiler_params=PARAMS,
        cost_estimate=pl.CostEstimate(flops=0, bytes_accessed=8_000_000, transcendentals=0),
    )(tile_source, tile_count, tiles)
    for step in range(ITERS):
        received = [lax.ppermute(sends[k], ("group", "dom"), route[k]) for k in range(PERMUTES)]
        total = pl.pallas_call(
            functools.partial(early_kernel, step == ITERS - 1),
            in_specs=[VMEM] * (5 + EARLY),
            out_specs=VMEM,
            out_shape=jax.ShapeDtypeStruct((classes, nodes), jnp.float32),
            compiler_params=PARAMS,
            cost_estimate=pl.CostEstimate(
                flops=2 * classes * nodes * (row_blocks + EARLY) * side,
                bytes_accessed=4_000_000,
                transcendentals=0,
            ),
        )(inv_root, seeds, soft, weight, own, *received[:EARLY])
        late = received[EARLY:]
        if step < ITERS - 1:
            own, *sends = pl.pallas_call(
                step_kernel,
                in_specs=[SMEM] + [VMEM] * (3 + len(late)),
                out_specs=[VMEM] * (1 + PERMUTES),
                out_shape=[wide] + narrow,
                compiler_params=PARAMS,
            )(send_list, inv_root, weight, total, *late)
    labels = pl.pallas_call(
        last_kernel,
        in_specs=[VMEM] * (3 + len(late)),
        out_specs=HBM,
        out_shape=jax.ShapeDtypeStruct((classes, nodes), jnp.float32),
        scratch_shapes=[
            pltpu.VMEM((classes, nodes), jnp.float32),
            pltpu.SemaphoreType.DMA((pieces,)),
        ],
        compiler_params=PARAMS,
    )(inv_root, weight, total, *late)
    return labels.T


def solution(mesh):
    return jax.shard_map(
        on_device,
        mesh=mesh,
        in_specs=(
            P(("group", "dom"), None),
            P(("group", "dom")),
            P(("group", "dom")),
            P(("group", "dom"), None, None, None),
            P(("group", "dom"), None),
            P(("group", "dom")),
            P(("group", "dom"), None),
        ),
        out_specs=P(("group", "dom"), None),
        check_vma=False,
    )
```

```python
import functools

import jax
import jax.numpy as jnp
from jax import lax
from jax.experimental import pallas as pl
from jax.experimental.pallas import tpu as pltpu
from jax.sharding import PartitionSpec as P

ITERS = 3
CORES = 2
ROW = 4
CHUNK = 256
SIDE = 128
SMEM = pl.BlockSpec(memory_space=pltpu.SMEM)
VMEM = pl.BlockSpec(memory_space=pltpu.VMEM)
HBM = pl.BlockSpec(memory_space=pltpu.HBM)
PARAMS = pltpu.CompilerParams(vmem_limit_bytes=40 * 1024 * 1024)

RING, EDGE, BACK, TWO, CROSS, UP, DOWN = range(7)
PERMUTES = 7
EARLY = 3


def routes(n_group, n_dom):
    def flat(g, d):
        return (g % n_group) * n_dom + d

    places = [(g, d) for g in range(n_group) for d in range(n_dom)]

    def ring(g, d):
        if g % CORES == 0:
            return (g, d + 1) if d % ROW < ROW - 1 else (g + 1, d)
        return (g, d - 1) if d % ROW > 0 else (g - 1, d)

    def pairs(distance, takes):
        both = []
        for g, d in places:
            if takes(d % ROW) and d + distance < n_dom:
                both += [(flat(g, d), flat(g, d + distance)), (flat(g, d + distance), flat(g, d))]
        return both

    forward = [(flat(*p), flat(*ring(*p))) for p in places]
    return {
        RING: forward,
        BACK: [(b, a) for a, b in forward],
        TWO: pairs(2, lambda x: x < 2),
        CROSS: pairs(2, lambda x: x >= 2),
        EDGE: pairs(1, lambda x: x == ROW - 1),
        UP: [(flat(g, d), flat(g + 1, d)) for g, d in places],
        DOWN: [(flat(g, d), flat(g - 1, d)) for g, d in places],
    }


def position():
    group, dom = lax.axis_index("group"), lax.axis_index("dom")
    return group, jnp.bitwise_and(group, CORES - 1), jnp.bitwise_and(dom, ROW - 1)


def columns_to_send():
    _, core, x = position()
    high = x >= 2
    return {
        RING: jnp.where(core == 0, 1, 0),
        BACK: jnp.where(core == 0, 0, 1),
        TWO: jnp.where(high, 2, 3),
        CROSS: jnp.where(high, 3, 2),
        EDGE: jnp.where(x == 0, 0, 1),
        UP: 5,
        DOWN: 4,
    }


def in_hbm(x):
    return pltpu.with_memory_space_constraint(x, pltpu.HBM)


def chunks(rows):
    return [(at, min(CHUNK, rows - at)) for at in range(0, rows, CHUNK)]


def put_sends(rows, send_ref, own_ref, send_refs):
    for k, column in columns_to_send().items():
        block = pl.ds(pl.multiple_of(send_ref[0, column] * SIDE, SIDE), SIDE)
        send_refs[k][rows, :] = own_ref[rows, block]


def start_of(rows, at, classes, seeds, prior_ref, columns=slice(None)):
    soft = prior_ref[rows, columns].astype(jnp.float32)
    label = lax.broadcasted_iota(jnp.int32, soft.shape, 0) + at
    return jnp.where(seeds < classes, jnp.where(label == seeds, 1.0, 0.0), soft)


def prepare_kernel(
    send_any, seeds_any, degree_any, prior_any, root_ref, seeds_ref, prior_ref, own_ref, *refs
):
    send_refs, (sends, seeds_held, degree_held, small, arrived) = refs[:PERMUTES], refs[PERMUTES:]
    classes, nodes = prior_any.shape
    firsts = [
        pltpu.make_async_copy(seeds_any, seeds_held, small.at[0]),
        pltpu.make_async_copy(degree_any, degree_held, small.at[1]),
        pltpu.make_async_copy(send_any, sends, small.at[2]),
    ]
    blocks = [pl.ds(at, SIDE) for at in range(0, nodes, SIDE)]
    copies = [
        pltpu.make_async_copy(prior_any.at[:, block], prior_ref.at[:, block], arrived.at[k])
        for k, block in enumerate(blocks)
    ]
    for copy in firsts + copies:
        copy.start()
    for copy in firsts:
        copy.wait()
    root_ref[...] = 1.0 / jnp.sqrt(degree_held[...].astype(jnp.float32)[None, :])
    seeds_ref[...] = seeds_held[...][None, :]
    for block, copy in zip(blocks, copies):
        copy.wait()
        seeds, inv_root = seeds_ref[:, block], root_ref[:, block]
        for at, size in chunks(classes):
            rows = pl.ds(at, size)
            start = start_of(rows, at, classes, seeds, prior_ref, block)
            own_ref[rows, block] = (inv_root * start).astype(jnp.bfloat16)
    for at, size in chunks(classes):
        put_sends(pl.ds(at, size), sends, own_ref, send_refs)


def gains(root_ref, last):
    inv_root = root_ref[...]
    if last:
        return 0.9 * inv_root, 0.1
    return inv_root * (0.9 * inv_root), 0.1 * inv_root


def early_kernel(last, root_ref, seeds_ref, prior_ref, weight_ref, own_ref, *refs):
    received, sum_ref = refs[:EARLY], refs[EARLY]
    depth = own_ref.shape[1] + EARLY * SIDE
    of_product, of_start = gains(root_ref, last)
    for at, size in chunks(own_ref.shape[0]):
        rows = pl.ds(at, size)
        sources = jnp.concatenate([own_ref[rows, :]] + [ref[rows, :] for ref in received], axis=1)
        product = jnp.dot(
            sources, weight_ref[pl.ds(0, depth), :], preferred_element_type=jnp.float32
        )
        start = start_of(rows, at, prior_ref.shape[0], seeds_ref[...], prior_ref)
        sum_ref[rows, :] = of_product * product + of_start * start


def finished(last, rows, root_ref, weight_ref, sum_ref, received):
    depth = len(received) * SIDE
    product = jnp.dot(
        jnp.concatenate([ref[rows, :] for ref in received], axis=1),
        weight_ref[pl.ds(weight_ref.shape[0] - depth, depth), :],
        preferred_element_type=jnp.float32,
    )
    return sum_ref[rows, :] + gains(root_ref, last)[0] * product


def step_kernel(send_ref, root_ref, weight_ref, sum_ref, *refs):
    late = PERMUTES - EARLY
    received, next_ref, send_refs = refs[:late], refs[late], refs[late + 1 :]
    for at, size in chunks(next_ref.shape[0]):
        rows = pl.ds(at, size)
        scaled = finished(False, rows, root_ref, weight_ref, sum_ref, received)
        next_ref[rows, :] = scaled.astype(jnp.bfloat16)
        put_sends(rows, send_ref, next_ref, send_refs)


def last_kernel(root_ref, weight_ref, sum_ref, *refs):
    late = PERMUTES - EARLY
    received, (out_ref, held, left) = refs[:late], refs[late:]
    copies = []
    for k, (at, size) in enumerate(chunks(held.shape[0])):
        rows = pl.ds(at, size)
        held[rows, :] = finished(True, rows, root_ref, weight_ref, sum_ref, received)
        copies.append(pltpu.make_async_copy(held.at[rows], out_ref.at[rows], left.at[k]))
        copies[-1].start()
    for copy in copies:
        copy.wait()


def weight_kernel(n_group, source_ref, count_ref, tiles_ref, weight_ref, total_ref):
    row_blocks, per_row, side, _ = tiles_ref.shape
    group, core, x = position()
    own = row_blocks
    place = [
        jnp.where(x == 0, own + EDGE, jnp.where(core == 0, own + RING, own + BACK)),
        jnp.where(x == ROW - 1, own + EDGE, jnp.where(core == 0, own + BACK, own + RING)),
        jnp.where(x >= 2, own + TWO, own + CROSS),
        jnp.where(x >= 2, own + CROSS, own + TWO),
        own + UP,
        own + DOWN,
    ]
    for r in range(row_blocks):
        total_ref[...] = jnp.zeros_like(total_ref)
        for t in range(per_row):
            source = source_ref[r, t]
            slot = source
            for k, where in enumerate(place):
                slot = jnp.where(source == own + k, where, slot)
            live = r * per_row + t < count_ref[0]
            live = live & ((source != own + 4) | (group > 0))
            live = live & ((source != own + 5) | (group < n_group - 1))

            @pl.when(live)
            def _():
                total_ref[slot] += tiles_ref[r, t].astype(jnp.float32)

        for s in range(own + PERMUTES):
            weight_ref[pl.ds(s * side, side), pl.ds(r * side, side)] = total_ref[s].T.astype(
                weight_ref.dtype
            )


def on_device(prior, seed_labels, degree, tiles, tile_source, tile_count, send_list):
    row_blocks, _, side, _ = tiles.shape
    nodes, classes = prior.shape
    n_group, n_dom = lax.axis_size("group"), lax.axis_size("dom")
    route = routes(n_group, n_dom)
    slots = row_blocks + PERMUTES
    pieces = len(chunks(classes))
    wide = jax.ShapeDtypeStruct((classes, nodes), jnp.bfloat16)
    narrow = [jax.ShapeDtypeStruct((classes, side), jnp.bfloat16)] * PERMUTES

    inv_root, seeds, soft, own, *sends = pl.pallas_call(
        prepare_kernel,
        in_specs=[HBM] * 4,
        out_specs=[VMEM] * (4 + PERMUTES),
        out_shape=[
            jax.ShapeDtypeStruct((1, nodes), jnp.float32),
            jax.ShapeDtypeStruct((1, nodes), jnp.int32),
            wide,
            wide,
        ]
        + narrow,
        scratch_shapes=[
            pltpu.SMEM(send_list.shape, jnp.int32),
            pltpu.VMEM((nodes,), jnp.int32),
            pltpu.VMEM((nodes,), jnp.int32),
            pltpu.SemaphoreType.DMA((3,)),
            pltpu.SemaphoreType.DMA((row_blocks,)),
        ],
        compiler_params=PARAMS,
    )(*[in_hbm(x) for x in (send_list, seed_labels, degree, prior.T)])
    weight = pl.pallas_call(
        functools.partial(weight_kernel, n_group),
        in_specs=[SMEM, SMEM, VMEM],
        out_specs=VMEM,
        out_shape=jax.ShapeDtypeStruct((slots * side, nodes), jnp.bfloat16),
        scratch_shapes=[pltpu.VMEM((slots, side, side), jnp.float32)],
        compiler_params=PARAMS,
        cost_estimate=pl.CostEstimate(flops=0, bytes_accessed=8_000_000, transcendentals=0),
    )(tile_source, tile_count, tiles)
    for step in range(ITERS):
        received = [lax.ppermute(sends[k], ("group", "dom"), route[k]) for k in range(PERMUTES)]
        total = pl.pallas_call(
            functools.partial(early_kernel, step == ITERS - 1),
            in_specs=[VMEM] * (5 + EARLY),
            out_specs=VMEM,
            out_shape=jax.ShapeDtypeStruct((classes, nodes), jnp.float32),
            compiler_params=PARAMS,
            cost_estimate=pl.CostEstimate(
                flops=2 * classes * nodes * (row_blocks + EARLY) * side,
                bytes_accessed=4_000_000,
                transcendentals=0,
            ),
        )(inv_root, seeds, soft, weight, own, *received[:EARLY])
        late = received[EARLY:]
        if step < ITERS - 1:
            own, *sends = pl.pallas_call(
                step_kernel,
                in_specs=[SMEM] + [VMEM] * (3 + len(late)),
                out_specs=[VMEM] * (1 + PERMUTES),
                out_shape=[wide] + narrow,
                compiler_params=PARAMS,
            )(send_list, inv_root, weight, total, *late)
    labels = pl.pallas_call(
        last_kernel,
        in_specs=[VMEM] * (3 + len(late)),
        out_specs=HBM,
        out_shape=jax.ShapeDtypeStruct((classes, nodes), jnp.float32),
        scratch_shapes=[
            pltpu.VMEM((classes, nodes), jnp.float32),
            pltpu.SemaphoreType.DMA((pieces,)),
        ],
        compiler_params=PARAMS,
    )(inv_root, weight, total, *late)
    return labels.T


def solution(mesh):
    return jax.shard_map(
        on_device,
        mesh=mesh,
        in_specs=(
            P(("group", "dom"), None),
            P(("group", "dom")),
            P(("group", "dom")),
            P(("group", "dom"), None, None, None),
            P(("group", "dom"), None),
            P(("group", "dom")),
            P(("group", "dom"), None),
        ),
        out_specs=P(("group", "dom"), None),
        check_vma=False,
    )
```

```python
import functools

import jax
import jax.numpy as jnp
from jax import lax
from jax.experimental import pallas as pl
from jax.experimental.pallas import tpu as pltpu
from jax.sharding import PartitionSpec as P

ITERS = 3
CORES = 2
ROW = 4
CHUNK = 256
SIDE = 128
SMEM = pl.BlockSpec(memory_space=pltpu.SMEM)
VMEM = pl.BlockSpec(memory_space=pltpu.VMEM)
HBM = pl.BlockSpec(memory_space=pltpu.HBM)
PARAMS = pltpu.CompilerParams(vmem_limit_bytes=40 * 1024 * 1024)

EDGE, RING, BACK, TWO, CROSS, UP, DOWN = range(7)
PERMUTES = 7
EARLY = 3


def routes(n_group, n_dom):
    def flat(g, d):
        return (g % n_group) * n_dom + d

    places = [(g, d) for g in range(n_group) for d in range(n_dom)]

    def ring(g, d):
        if g % CORES == 0:
            return (g, d + 1) if d % ROW < ROW - 1 else (g + 1, d)
        return (g, d - 1) if d % ROW > 0 else (g - 1, d)

    def pairs(distance, takes):
        both = []
        for g, d in places:
            if takes(d % ROW) and d + distance < n_dom:
                both += [(flat(g, d), flat(g, d + distance)), (flat(g, d + distance), flat(g, d))]
        return both

    forward = [(flat(*p), flat(*ring(*p))) for p in places]
    return {
        RING: forward,
        BACK: [(b, a) for a, b in forward],
        TWO: pairs(2, lambda x: x < 2),
        CROSS: pairs(2, lambda x: x >= 2),
        EDGE: pairs(1, lambda x: x == ROW - 1),
        UP: [(flat(g, d), flat(g + 1, d)) for g, d in places],
        DOWN: [(flat(g, d), flat(g - 1, d)) for g, d in places],
    }


def position():
    group, dom = lax.axis_index("group"), lax.axis_index("dom")
    return group, jnp.bitwise_and(group, CORES - 1), jnp.bitwise_and(dom, ROW - 1)


def columns_to_send():
    _, core, x = position()
    high = x >= 2
    return {
        RING: jnp.where(core == 0, 1, 0),
        BACK: jnp.where(core == 0, 0, 1),
        TWO: jnp.where(high, 2, 3),
        CROSS: jnp.where(high, 3, 2),
        EDGE: jnp.where(x == 0, 0, 1),
        UP: 5,
        DOWN: 4,
    }


def in_hbm(x):
    return pltpu.with_memory_space_constraint(x, pltpu.HBM)


def chunks(rows):
    return [(at, min(CHUNK, rows - at)) for at in range(0, rows, CHUNK)]


def put_sends(rows, send_ref, own_ref, send_refs):
    for k, column in columns_to_send().items():
        block = pl.ds(pl.multiple_of(send_ref[0, column] * SIDE, SIDE), SIDE)
        send_refs[k][rows, :] = own_ref[rows, block]


def start_of(rows, at, classes, seeds, prior_ref, columns=slice(None)):
    soft = prior_ref[rows, columns].astype(jnp.float32)
    label = lax.broadcasted_iota(jnp.int32, soft.shape, 0) + at
    return jnp.where(seeds < classes, jnp.where(label == seeds, 1.0, 0.0), soft)


def prepare_kernel(
    send_any, seeds_any, degree_any, prior_any, root_ref, seeds_ref, prior_ref, own_ref, *refs
):
    send_refs, (sends, seeds_held, degree_held, small, arrived) = refs[:PERMUTES], refs[PERMUTES:]
    classes, nodes = prior_any.shape
    firsts = [
        pltpu.make_async_copy(seeds_any, seeds_held, small.at[0]),
        pltpu.make_async_copy(degree_any, degree_held, small.at[1]),
        pltpu.make_async_copy(send_any, sends, small.at[2]),
    ]
    blocks = [pl.ds(at, SIDE) for at in range(0, nodes, SIDE)]
    copies = [
        pltpu.make_async_copy(prior_any.at[:, block], prior_ref.at[:, block], arrived.at[k])
        for k, block in enumerate(blocks)
    ]
    for copy in firsts + copies:
        copy.start()
    for copy in firsts:
        copy.wait()
    root_ref[...] = 1.0 / jnp.sqrt(degree_held[...].astype(jnp.float32)[None, :])
    seeds_ref[...] = seeds_held[...][None, :]
    for block, copy in zip(blocks, copies):
        copy.wait()
        seeds, inv_root = seeds_ref[:, block], root_ref[:, block]
        for at, size in chunks(classes):
            rows = pl.ds(at, size)
            start = start_of(rows, at, classes, seeds, prior_ref, block)
            own_ref[rows, block] = (inv_root * start).astype(jnp.bfloat16)
    for at, size in chunks(classes):
        put_sends(pl.ds(at, size), sends, own_ref, send_refs)


def gains(root_ref, last):
    inv_root = root_ref[...]
    if last:
        return 0.9 * inv_root, 0.1
    return inv_root * (0.9 * inv_root), 0.1 * inv_root


def early_kernel(last, root_ref, seeds_ref, prior_ref, weight_ref, own_ref, *refs):
    received, sum_ref = refs[:EARLY], refs[EARLY]
    depth = own_ref.shape[1] + EARLY * SIDE
    of_product, of_start = gains(root_ref, last)
    for at, size in chunks(own_ref.shape[0]):
        rows = pl.ds(at, size)
        sources = jnp.concatenate([own_ref[rows, :]] + [ref[rows, :] for ref in received], axis=1)
        product = jnp.dot(
            sources, weight_ref[pl.ds(0, depth), :], preferred_element_type=jnp.float32
        )
        start = start_of(rows, at, prior_ref.shape[0], seeds_ref[...], prior_ref)
        sum_ref[rows, :] = of_product * product + of_start * start


def finished(last, rows, root_ref, weight_ref, sum_ref, received):
    depth = len(received) * SIDE
    product = jnp.dot(
        jnp.concatenate([ref[rows, :] for ref in received], axis=1),
        weight_ref[pl.ds(weight_ref.shape[0] - depth, depth), :],
        preferred_element_type=jnp.float32,
    )
    return sum_ref[rows, :] + gains(root_ref, last)[0] * product


def step_kernel(send_ref, root_ref, weight_ref, sum_ref, *refs):
    late = PERMUTES - EARLY
    received, next_ref, send_refs = refs[:late], refs[late], refs[late + 1 :]
    for at, size in chunks(next_ref.shape[0]):
        rows = pl.ds(at, size)
        scaled = finished(False, rows, root_ref, weight_ref, sum_ref, received)
        next_ref[rows, :] = scaled.astype(jnp.bfloat16)
        put_sends(rows, send_ref, next_ref, send_refs)


def last_kernel(root_ref, weight_ref, sum_ref, *refs):
    late = PERMUTES - EARLY
    received, (out_ref, held, left) = refs[:late], refs[late:]
    copies = []
    for k, (at, size) in enumerate(chunks(held.shape[0])):
        rows = pl.ds(at, size)
        held[rows, :] = finished(True, rows, root_ref, weight_ref, sum_ref, received)
        copies.append(pltpu.make_async_copy(held.at[rows], out_ref.at[rows], left.at[k]))
        copies[-1].start()
    for copy in copies:
        copy.wait()


def weight_kernel(n_group, source_ref, count_ref, tiles_ref, weight_ref, total_ref):
    row_blocks, per_row, side, _ = tiles_ref.shape
    group, core, x = position()
    own = row_blocks
    place = [
        jnp.where(x == 0, own + EDGE, jnp.where(core == 0, own + RING, own + BACK)),
        jnp.where(x == ROW - 1, own + EDGE, jnp.where(core == 0, own + BACK, own + RING)),
        jnp.where(x >= 2, own + TWO, own + CROSS),
        jnp.where(x >= 2, own + CROSS, own + TWO),
        own + UP,
        own + DOWN,
    ]
    for r in range(row_blocks):
        total_ref[...] = jnp.zeros_like(total_ref)
        for t in range(per_row):
            source = source_ref[r, t]
            slot = source
            for k, where in enumerate(place):
                slot = jnp.where(source == own + k, where, slot)
            live = r * per_row + t < count_ref[0]
            live = live & ((source != own + 4) | (group > 0))
            live = live & ((source != own + 5) | (group < n_group - 1))

            @pl.when(live)
            def _():
                total_ref[slot] += tiles_ref[r, t].astype(jnp.float32)

        for s in range(own + PERMUTES):
            weight_ref[pl.ds(s * side, side), pl.ds(r * side, side)] = total_ref[s].T.astype(
                weight_ref.dtype
            )


def on_device(prior, seed_labels, degree, tiles, tile_source, tile_count, send_list):
    row_blocks, _, side, _ = tiles.shape
    nodes, classes = prior.shape
    n_group, n_dom = lax.axis_size("group"), lax.axis_size("dom")
    route = routes(n_group, n_dom)
    slots = row_blocks + PERMUTES
    pieces = len(chunks(classes))
    wide = jax.ShapeDtypeStruct((classes, nodes), jnp.bfloat16)
    narrow = [jax.ShapeDtypeStruct((classes, side), jnp.bfloat16)] * PERMUTES

    inv_root, seeds, soft, own, *sends = pl.pallas_call(
        prepare_kernel,
        in_specs=[HBM] * 4,
        out_specs=[VMEM] * (4 + PERMUTES),
        out_shape=[
            jax.ShapeDtypeStruct((1, nodes), jnp.float32),
            jax.ShapeDtypeStruct((1, nodes), jnp.int32),
            wide,
            wide,
        ]
        + narrow,
        scratch_shapes=[
            pltpu.SMEM(send_list.shape, jnp.int32),
            pltpu.VMEM((nodes,), jnp.int32),
            pltpu.VMEM((nodes,), jnp.int32),
            pltpu.SemaphoreType.DMA((3,)),
            pltpu.SemaphoreType.DMA((row_blocks,)),
        ],
        compiler_params=PARAMS,
    )(*[in_hbm(x) for x in (send_list, seed_labels, degree, prior.T)])
    weight = pl.pallas_call(
        functools.partial(weight_kernel, n_group),
        in_specs=[SMEM, SMEM, VMEM],
        out_specs=VMEM,
        out_shape=jax.ShapeDtypeStruct((slots * side, nodes), jnp.bfloat16),
        scratch_shapes=[pltpu.VMEM((slots, side, side), jnp.float32)],
        compiler_params=PARAMS,
        cost_estimate=pl.CostEstimate(flops=0, bytes_accessed=8_000_000, transcendentals=0),
    )(tile_source, tile_count, tiles)
    for step in range(ITERS):
        received = [lax.ppermute(sends[k], ("group", "dom"), route[k]) for k in range(PERMUTES)]
        total = pl.pallas_call(
            functools.partial(early_kernel, step == ITERS - 1),
            in_specs=[VMEM] * (5 + EARLY),
            out_specs=VMEM,
            out_shape=jax.ShapeDtypeStruct((classes, nodes), jnp.float32),
            compiler_params=PARAMS,
            cost_estimate=pl.CostEstimate(
                flops=2 * classes * nodes * (row_blocks + EARLY) * side,
                bytes_accessed=4_000_000,
                transcendentals=0,
            ),
        )(inv_root, seeds, soft, weight, own, *received[:EARLY])
        late = received[EARLY:]
        if step < ITERS - 1:
            own, *sends = pl.pallas_call(
                step_kernel,
                in_specs=[SMEM] + [VMEM] * (3 + len(late)),
                out_specs=[VMEM] * (1 + PERMUTES),
                out_shape=[wide] + narrow,
                compiler_params=PARAMS,
            )(send_list, inv_root, weight, total, *late)
    labels = pl.pallas_call(
        last_kernel,
        in_specs=[VMEM] * (3 + len(late)),
        out_specs=HBM,
        out_shape=jax.ShapeDtypeStruct((classes, nodes), jnp.float32),
        scratch_shapes=[
            pltpu.VMEM((classes, nodes), jnp.float32),
            pltpu.SemaphoreType.DMA((pieces,)),
        ],
        compiler_params=PARAMS,
    )(inv_root, weight, total, *late)
    return labels.T


def solution(mesh):
    return jax.shard_map(
        on_device,
        mesh=mesh,
        in_specs=(
            P(("group", "dom"), None),
            P(("group", "dom")),
            P(("group", "dom")),
            P(("group", "dom"), None, None, None),
            P(("group", "dom"), None),
            P(("group", "dom")),
            P(("group", "dom"), None),
        ),
        out_specs=P(("group", "dom"), None),
        check_vma=False,
    )
```

```python
import functools

import jax
import jax.numpy as jnp
from jax import lax
from jax.experimental import pallas as pl
from jax.experimental.pallas import tpu as pltpu
from jax.sharding import PartitionSpec as P

ITERS = 3
CORES = 2
ROW = 4
CHUNK = 256
SIDE = 128
SMEM = pl.BlockSpec(memory_space=pltpu.SMEM)
VMEM = pl.BlockSpec(memory_space=pltpu.VMEM)
HBM = pl.BlockSpec(memory_space=pltpu.HBM)
PARAMS = pltpu.CompilerParams(vmem_limit_bytes=40 * 1024 * 1024)

BACK, EDGE, RING, TWO, CROSS, UP, DOWN = range(7)
PERMUTES = 7
EARLY = 3


def routes(n_group, n_dom):
    def flat(g, d):
        return (g % n_group) * n_dom + d

    places = [(g, d) for g in range(n_group) for d in range(n_dom)]

    def ring(g, d):
        if g % CORES == 0:
            return (g, d + 1) if d % ROW < ROW - 1 else (g + 1, d)
        return (g, d - 1) if d % ROW > 0 else (g - 1, d)

    def pairs(distance, takes):
        both = []
        for g, d in places:
            if takes(d % ROW) and d + distance < n_dom:
                both += [(flat(g, d), flat(g, d + distance)), (flat(g, d + distance), flat(g, d))]
        return both

    forward = [(flat(*p), flat(*ring(*p))) for p in places]
    return {
        RING: forward,
        BACK: [(b, a) for a, b in forward],
        TWO: pairs(2, lambda x: x < 2),
        CROSS: pairs(2, lambda x: x >= 2),
        EDGE: pairs(1, lambda x: x == ROW - 1),
        UP: [(flat(g, d), flat(g + 1, d)) for g, d in places],
        DOWN: [(flat(g, d), flat(g - 1, d)) for g, d in places],
    }


def position():
    group, dom = lax.axis_index("group"), lax.axis_index("dom")
    return group, jnp.bitwise_and(group, CORES - 1), jnp.bitwise_and(dom, ROW - 1)


def columns_to_send():
    _, core, x = position()
    high = x >= 2
    return {
        RING: jnp.where(core == 0, 1, 0),
        BACK: jnp.where(core == 0, 0, 1),
        TWO: jnp.where(high, 2, 3),
        CROSS: jnp.where(high, 3, 2),
        EDGE: jnp.where(x == 0, 0, 1),
        UP: 5,
        DOWN: 4,
    }


def in_hbm(x):
    return pltpu.with_memory_space_constraint(x, pltpu.HBM)


def chunks(rows):
    return [(at, min(CHUNK, rows - at)) for at in range(0, rows, CHUNK)]


def put_sends(rows, send_ref, own_ref, send_refs):
    for k, column in columns_to_send().items():
        block = pl.ds(pl.multiple_of(send_ref[0, column] * SIDE, SIDE), SIDE)
        send_refs[k][rows, :] = own_ref[rows, block]


def start_of(rows, at, classes, seeds, prior_ref, columns=slice(None)):
    soft = prior_ref[rows, columns].astype(jnp.float32)
    label = lax.broadcasted_iota(jnp.int32, soft.shape, 0) + at
    return jnp.where(seeds < classes, jnp.where(label == seeds, 1.0, 0.0), soft)


def prepare_kernel(
    send_any, seeds_any, degree_any, prior_any, root_ref, seeds_ref, prior_ref, own_ref, *refs
):
    send_refs, (sends, seeds_held, degree_held, small, arrived) = refs[:PERMUTES], refs[PERMUTES:]
    classes, nodes = prior_any.shape
    firsts = [
        pltpu.make_async_copy(seeds_any, seeds_held, small.at[0]),
        pltpu.make_async_copy(degree_any, degree_held, small.at[1]),
        pltpu.make_async_copy(send_any, sends, small.at[2]),
    ]
    blocks = [pl.ds(at, SIDE) for at in range(0, nodes, SIDE)]
    copies = [
        pltpu.make_async_copy(prior_any.at[:, block], prior_ref.at[:, block], arrived.at[k])
        for k, block in enumerate(blocks)
    ]
    for copy in firsts + copies:
        copy.start()
    for copy in firsts:
        copy.wait()
    root_ref[...] = 1.0 / jnp.sqrt(degree_held[...].astype(jnp.float32)[None, :])
    seeds_ref[...] = seeds_held[...][None, :]
    for block, copy in zip(blocks, copies):
        copy.wait()
        seeds, inv_root = seeds_ref[:, block], root_ref[:, block]
        for at, size in chunks(classes):
            rows = pl.ds(at, size)
            start = start_of(rows, at, classes, seeds, prior_ref, block)
            own_ref[rows, block] = (inv_root * start).astype(jnp.bfloat16)
    for at, size in chunks(classes):
        put_sends(pl.ds(at, size), sends, own_ref, send_refs)


def gains(root_ref, last):
    inv_root = root_ref[...]
    if last:
        return 0.9 * inv_root, 0.1
    return inv_root * (0.9 * inv_root), 0.1 * inv_root


def early_kernel(last, root_ref, seeds_ref, prior_ref, weight_ref, own_ref, *refs):
    received, sum_ref = refs[:EARLY], refs[EARLY]
    depth = own_ref.shape[1] + EARLY * SIDE
    of_product, of_start = gains(root_ref, last)
    for at, size in chunks(own_ref.shape[0]):
        rows = pl.ds(at, size)
        sources = jnp.concatenate([own_ref[rows, :]] + [ref[rows, :] for ref in received], axis=1)
        product = jnp.dot(
            sources, weight_ref[pl.ds(0, depth), :], preferred_element_type=jnp.float32
        )
        start = start_of(rows, at, prior_ref.shape[0], seeds_ref[...], prior_ref)
        sum_ref[rows, :] = of_product * product + of_start * start


def finished(last, rows, root_ref, weight_ref, sum_ref, received):
    depth = len(received) * SIDE
    product = jnp.dot(
        jnp.concatenate([ref[rows, :] for ref in received], axis=1),
        weight_ref[pl.ds(weight_ref.shape[0] - depth, depth), :],
        preferred_element_type=jnp.float32,
    )
    return sum_ref[rows, :] + gains(root_ref, last)[0] * product


def step_kernel(send_ref, root_ref, weight_ref, sum_ref, *refs):
    late = PERMUTES - EARLY
    received, next_ref, send_refs = refs[:late], refs[late], refs[late + 1 :]
    for at, size in chunks(next_ref.shape[0]):
        rows = pl.ds(at, size)
        scaled = finished(False, rows, root_ref, weight_ref, sum_ref, received)
        next_ref[rows, :] = scaled.astype(jnp.bfloat16)
        put_sends(rows, send_ref, next_ref, send_refs)


def last_kernel(root_ref, weight_ref, sum_ref, *refs):
    late = PERMUTES - EARLY
    received, (out_ref, held, left) = refs[:late], refs[late:]
    copies = []
    for k, (at, size) in enumerate(chunks(held.shape[0])):
        rows = pl.ds(at, size)
        held[rows, :] = finished(True, rows, root_ref, weight_ref, sum_ref, received)
        copies.append(pltpu.make_async_copy(held.at[rows], out_ref.at[rows], left.at[k]))
        copies[-1].start()
    for copy in copies:
        copy.wait()


def weight_kernel(n_group, source_ref, count_ref, tiles_ref, weight_ref, total_ref):
    row_blocks, per_row, side, _ = tiles_ref.shape
    group, core, x = position()
    own = row_blocks
    place = [
        jnp.where(x == 0, own + EDGE, jnp.where(core == 0, own + RING, own + BACK)),
        jnp.where(x == ROW - 1, own + EDGE, jnp.where(core == 0, own + BACK, own + RING)),
        jnp.where(x >= 2, own + TWO, own + CROSS),
        jnp.where(x >= 2, own + CROSS, own + TWO),
        own + UP,
        own + DOWN,
    ]
    for r in range(row_blocks):
        total_ref[...] = jnp.zeros_like(total_ref)
        for t in range(per_row):
            source = source_ref[r, t]
            slot = source
            for k, where in enumerate(place):
                slot = jnp.where(source == own + k, where, slot)
            live = r * per_row + t < count_ref[0]
            live = live & ((source != own + 4) | (group > 0))
            live = live & ((source != own + 5) | (group < n_group - 1))

            @pl.when(live)
            def _():
                total_ref[slot] += tiles_ref[r, t].astype(jnp.float32)

        for s in range(own + PERMUTES):
            weight_ref[pl.ds(s * side, side), pl.ds(r * side, side)] = total_ref[s].T.astype(
                weight_ref.dtype
            )


def on_device(prior, seed_labels, degree, tiles, tile_source, tile_count, send_list):
    row_blocks, _, side, _ = tiles.shape
    nodes, classes = prior.shape
    n_group, n_dom = lax.axis_size("group"), lax.axis_size("dom")
    route = routes(n_group, n_dom)
    slots = row_blocks + PERMUTES
    pieces = len(chunks(classes))
    wide = jax.ShapeDtypeStruct((classes, nodes), jnp.bfloat16)
    narrow = [jax.ShapeDtypeStruct((classes, side), jnp.bfloat16)] * PERMUTES

    inv_root, seeds, soft, own, *sends = pl.pallas_call(
        prepare_kernel,
        in_specs=[HBM] * 4,
        out_specs=[VMEM] * (4 + PERMUTES),
        out_shape=[
            jax.ShapeDtypeStruct((1, nodes), jnp.float32),
            jax.ShapeDtypeStruct((1, nodes), jnp.int32),
            wide,
            wide,
        ]
        + narrow,
        scratch_shapes=[
            pltpu.SMEM(send_list.shape, jnp.int32),
            pltpu.VMEM((nodes,), jnp.int32),
            pltpu.VMEM((nodes,), jnp.int32),
            pltpu.SemaphoreType.DMA((3,)),
            pltpu.SemaphoreType.DMA((row_blocks,)),
        ],
        compiler_params=PARAMS,
    )(*[in_hbm(x) for x in (send_list, seed_labels, degree, prior.T)])
    weight = pl.pallas_call(
        functools.partial(weight_kernel, n_group),
        in_specs=[SMEM, SMEM, VMEM],
        out_specs=VMEM,
        out_shape=jax.ShapeDtypeStruct((slots * side, nodes), jnp.bfloat16),
        scratch_shapes=[pltpu.VMEM((slots, side, side), jnp.float32)],
        compiler_params=PARAMS,
        cost_estimate=pl.CostEstimate(flops=0, bytes_accessed=8_000_000, transcendentals=0),
    )(tile_source, tile_count, tiles)
    for step in range(ITERS):
        received = [lax.ppermute(sends[k], ("group", "dom"), route[k]) for k in range(PERMUTES)]
        total = pl.pallas_call(
            functools.partial(early_kernel, step == ITERS - 1),
            in_specs=[VMEM] * (5 + EARLY),
            out_specs=VMEM,
            out_shape=jax.ShapeDtypeStruct((classes, nodes), jnp.float32),
            compiler_params=PARAMS,
            cost_estimate=pl.CostEstimate(
                flops=2 * classes * nodes * (row_blocks + EARLY) * side,
                bytes_accessed=4_000_000,
                transcendentals=0,
            ),
        )(inv_root, seeds, soft, weight, own, *received[:EARLY])
        late = received[EARLY:]
        if step < ITERS - 1:
            own, *sends = pl.pallas_call(
                step_kernel,
                in_specs=[SMEM] + [VMEM] * (3 + len(late)),
                out_specs=[VMEM] * (1 + PERMUTES),
                out_shape=[wide] + narrow,
                compiler_params=PARAMS,
            )(send_list, inv_root, weight, total, *late)
    labels = pl.pallas_call(
        last_kernel,
        in_specs=[VMEM] * (3 + len(late)),
        out_specs=HBM,
        out_shape=jax.ShapeDtypeStruct((classes, nodes), jnp.float32),
        scratch_shapes=[
            pltpu.VMEM((classes, nodes), jnp.float32),
            pltpu.SemaphoreType.DMA((pieces,)),
        ],
        compiler_params=PARAMS,
    )(inv_root, weight, total, *late)
    return labels.T


def solution(mesh):
    return jax.shard_map(
        on_device,
        mesh=mesh,
        in_specs=(
            P(("group", "dom"), None),
            P(("group", "dom")),
            P(("group", "dom")),
            P(("group", "dom"), None, None, None),
            P(("group", "dom"), None),
            P(("group", "dom")),
            P(("group", "dom"), None),
        ),
        out_specs=P(("group", "dom"), None),
        check_vma=False,
    )
```
